32 devices in a mesh: rep: 2 (over y), grp: 2 (over core), blk: 8 (over z, x).
Axes of the slice: x: 2, y: 2, z: 4, core: 2. Of those that a mesh axis runs over, the one named last changes fastest.
Arguments:
- queries: bfloat16 [2048, 8, 576], P(('rep', 'grp'), 'blk'), parts along dimension 0, may hold values from -64 to 64
- latents: bfloat16 [2048, 576], P(('rep', 'grp', 'blk')), parts along dimension 0, may hold values from -12 to 12
- out_grad: bfloat16 [2048, 8, 512], P(('rep', 'grp'), 'blk'), parts along dimension 0, may hold values from -6 to 6
- first_key: int32 [2048], P(('rep', 'grp')), parts along dimension 0, may hold values from 0 to 127, as said below
Outputs:
- query_grad: bfloat16 [2048, 8, 576], P(('rep', 'grp'), 'blk'), parts along dimension 0
- latent_grad: bfloat16 [2048, 576], P(('rep', 'grp', 'blk')), parts along dimension 0
The draws below stay inside these ranges and needn't reach their ends.
There are 2 independent parts, one for each index of `rep`. The reference program is written for one: setup_inputs(seed, part) draws one part's arguments, and reference() takes and returns one part's arrays. A program takes and returns all parts, laid end to end along the dimension named above; each array names one. Nothing has to cross between parts.
Inputs may be any that keep to these rules, and one draw needn't show every extreme that they name: `first_key`: 0 for tokens of the first block; for a token of block b >= 1 a position among the first 128 of block b - 1.
All inputs are finite; a program needn't handle non-finite values.
Results may differ from the reference program's by a relative error of at most 0.0055.
Values may be sent and summed in bfloat16 or wider, within the bound.
A program may use at most 64 MiB of HBM per device.

```python
import jax
import jax.numpy as jnp
from jax import lax

RANK = 512
BLOCK = 512
H = 8
LAT = 576
TOKENS = 1024


def latent_pair(key):
    base = jnp.clip(jax.random.normal(jax.random.fold_in(key, 101), (TOKENS, LAT), jnp.float32), -6.0, 6.0)
    queries = jnp.clip(jax.random.normal(jax.random.fold_in(key, 105), (TOKENS, H, LAT), jnp.float32), -6.0, 6.0) * 0.5
    bound = 64.0 * 576.0 / LAT
    queries = jnp.clip(queries, -bound, bound)
    return (base, queries)


def draw_latents(key, part):
    return latent_pair(key)[0].astype(jnp.bfloat16)


def draw_queries(key, part):
    return latent_pair(key)[1].astype(jnp.bfloat16)


def draw_first_key(key, part):
    positions = jnp.arange(TOKENS, dtype=jnp.int32)
    group_of = positions // BLOCK
    offsets = jax.random.randint(jax.random.fold_in(key, 201), (TOKENS,), 0, BLOCK // 4, jnp.int32)
    values = jnp.where(group_of >= 1, (group_of - 1) * BLOCK + offsets, 0)
    values = jnp.where(positions == TOKENS - BLOCK, TOKENS - 2 * BLOCK + BLOCK // 4 - 1, values)
    return values.astype(jnp.int32)


def strengthened(result, stream_key, source, target, blocks, factor):
    owner, partner = [(jnp.arange(result.shape[axis_at]) // (result.shape[axis_at] // blocks)).reshape([-1 if axis == axis_at else 1 for axis in range(result.ndim)]) for axis_at in (source, target)]
    chosen = jax.random.permutation(stream_key, blocks)[partner]
    strong = (owner == chosen) | (owner == (partner + blocks // 2) % blocks)
    return jnp.where(strong, factor * result, result)


def steps_of(key, shape, shards, low, top_value):
    def one(axis_at, blocks):
        heights = jax.random.uniform(jax.random.fold_in(jax.random.fold_in(key, 6), axis_at), (blocks,), jnp.float32, low / len(shards), top_value / len(shards))
        return jnp.repeat(jnp.exp(heights), shape[axis_at] // blocks).reshape((-1,) + (1,) * (len(shape) - axis_at - 1))

    gain = one(*shards[0])
    for cut in shards[1:]:
        gain = gain * one(*cut)
    return gain


def bell_draw_with(own_key, dims, scale, most, shards, heavy, kind=jnp.bfloat16):
    drawn = scale * jax.random.normal(own_key, dims, jnp.float32)
    if shards:
        drawn = drawn * steps_of(own_key, dims, shards, -0.22, 0.18)
    return jnp.clip(strengthened(drawn, jax.random.fold_in(own_key, 3), *heavy), -most, most).astype(kind)


def setup_inputs(seed: int = 0, part: int = 0) -> dict:
    streams_of = jax.random.split(jax.random.key(seed), 5)
    part_splits = jax.random.split(jax.random.fold_in(streams_of[4], part), 5)
    queries = draw_queries(jax.random.fold_in(jax.random.fold_in(streams_of[4], part), 71), part)
    latents = draw_latents(jax.random.fold_in(jax.random.fold_in(streams_of[4], part), 71), part)
    out_grad = bell_draw_with(part_splits[2], (TOKENS, H, RANK), 1.0, 6.0, ((0, 2), (1, 8)), (1, 0, 8, 2.0))
    first_key = draw_first_key(jax.random.fold_in(jax.random.fold_in(streams_of[4], part), 71), part)
    return dict(queries=queries, latents=latents, out_grad=out_grad, first_key=first_key)


score_scale = 192.0 ** -0.5


def attend_grads(query_blk, grad_blk, key_rows, visible):
    count, head_count, width = query_blk.shape
    query_rows = query_blk.reshape(count * head_count, width)
    grad_rows = grad_blk.reshape(count * head_count, -1)
    rank_width = grad_rows.shape[1]
    value_rows = key_rows[:, :rank_width]
    scores = jnp.dot(query_rows, key_rows.T, preferred_element_type=jnp.float32) * score_scale
    scores = scores.reshape(count, head_count, -1)
    mask_three = visible[:, None, :]
    row_max = jnp.max(jnp.where(mask_three, scores, -jnp.inf), axis=-1, keepdims=True)
    total = jnp.sum(jnp.where(mask_three, jnp.exp(scores - row_max), 0.0), axis=-1, keepdims=True)
    log_norm = row_max + jnp.log(total)
    attn_probs = jnp.where(mask_three, jnp.exp(scores - log_norm), 0.0).astype(jnp.bfloat16)
    attn_probs = attn_probs.reshape(count * head_count, -1)
    outputs = jnp.dot(attn_probs, value_rows, preferred_element_type=jnp.float32)
    row_delta = jnp.sum(grad_rows.astype(jnp.float32) * outputs, axis=-1, keepdims=True)
    prob_grad = jnp.dot(grad_rows, value_rows.T, preferred_element_type=jnp.float32)
    score_grad = (attn_probs.astype(jnp.float32) * (prob_grad - row_delta) * score_scale).astype(jnp.bfloat16)
    query_grad = jnp.dot(score_grad, key_rows, preferred_element_type=jnp.float32).astype(jnp.bfloat16)
    latent_part = jnp.dot(score_grad.T, query_rows, preferred_element_type=jnp.float32)
    value_part = jnp.dot(attn_probs.T, grad_rows, preferred_element_type=jnp.float32)
    latent_part = jnp.concatenate([latent_part[:, :rank_width] + value_part, latent_part[:, rank_width:]], axis=1)
    return query_grad.reshape(count, head_count, width), latent_part


def reference(queries, latents, out_grad, first_key):
    block_len = BLOCK
    group_total = TOKENS // block_len
    per_step = 8
    steps_count = block_len // per_step
    grad_total = jnp.zeros((TOKENS, LAT), jnp.float32)
    query_parts = []
    for group_id in range(group_total):
        start = group_id * block_len
        own_block = latents[start:start + block_len]
        if group_id > 0:
            prev_block = latents[start - block_len:start]
        else:
            prev_block = jnp.zeros_like(own_block)
        key_rows = jnp.concatenate([prev_block, own_block], axis=0)
        key_pos = (jnp.arange(2 * block_len, dtype=jnp.int32) + (start - block_len)).astype(jnp.int32)
        in_prev = jnp.arange(2 * block_len, dtype=jnp.int32) < block_len
        query_groups = queries[start:start + block_len].reshape(steps_count, per_step, H, LAT)
        grad_groups = out_grad[start:start + block_len].reshape(steps_count, per_step, H, RANK)
        first_groups = first_key[start:start + block_len].reshape(steps_count, per_step)
        pos_groups = (jnp.arange(block_len, dtype=jnp.int32) + start).reshape(steps_count, per_step)

        def scan_step(carry, items):
            query_blk, grad_blk, first_blk, pos_blk = items
            prev_ok = (key_pos[None, :] >= first_blk[:, None]) & (group_id > 0)
            own_ok = key_pos[None, :] <= pos_blk[:, None]
            visible = jnp.where(in_prev[None, :], prev_ok, own_ok)
            query_grad, latent_part = attend_grads(query_blk, grad_blk, key_rows, visible)
            return carry + latent_part, query_grad

        carry_init = jnp.zeros((2 * block_len, LAT), jnp.float32)
        latent_acc, query_blocks = lax.scan(scan_step, carry_init, (query_groups, grad_groups, first_groups, pos_groups))
        query_parts.append(query_blocks.reshape(block_len, H, LAT))
        grad_total = grad_total.at[start:start + block_len].add(latent_acc[block_len:])
        if group_id > 0:
            grad_total = grad_total.at[start - block_len:start].add(latent_acc[:block_len])
    query_grad = jnp.concatenate(query_parts, axis=0)
    return query_grad, grad_total.astype(jnp.bfloat16)
```

```python
import functools

import jax
import jax.numpy as jnp
from jax import lax
from jax.experimental import pallas as pl
from jax.experimental.pallas import tpu as pltpu
from jax.sharding import PartitionSpec as P

score_scale = 192.0 ** (-0.5)


def shifted(shard, axis, by):
    count = lax.axis_size(axis)
    pairs = [(i, i + by) for i in range(count) if 0 <= i + by < count]
    return lax.ppermute(shard, axis, pairs)


def attend_grads(query_blk, grad_blk, key_rows, visible):
    count, head_count, width = query_blk.shape
    query_rows = query_blk.reshape(count * head_count, width)
    grad_rows = grad_blk.reshape(count * head_count, -1)
    rank_width = grad_rows.shape[1]
    value_rows = key_rows[:, :rank_width]
    scores = jnp.dot(query_rows, key_rows.T, preferred_element_type=jnp.float32) * score_scale
    scores = scores.reshape(count, head_count, -1)
    mask_three = visible[:, None, :]
    row_max = jnp.max(jnp.where(mask_three, scores, -jnp.inf), axis=-1, keepdims=True)
    total = jnp.sum(jnp.where(mask_three, jnp.exp(scores - row_max), 0.0), axis=-1, keepdims=True)
    log_norm = row_max + jnp.log(total)
    attn_probs = jnp.where(mask_three, jnp.exp(scores - log_norm), 0.0).astype(jnp.bfloat16)
    attn_probs = attn_probs.reshape(count * head_count, -1)
    outputs = jnp.dot(attn_probs, value_rows, preferred_element_type=jnp.float32)
    row_delta = jnp.sum(grad_rows.astype(jnp.float32) * outputs, axis=-1, keepdims=True)
    prob_grad = jnp.dot(grad_rows, value_rows.T, preferred_element_type=jnp.float32)
    score_grad = (attn_probs.astype(jnp.float32) * (prob_grad - row_delta) * score_scale).astype(
        jnp.bfloat16
    )
    query_grad = jnp.dot(score_grad, key_rows, preferred_element_type=jnp.float32).astype(
        jnp.bfloat16
    )
    latent_part = jnp.dot(score_grad.T, query_rows, preferred_element_type=jnp.float32)
    value_part = jnp.dot(attn_probs.T, grad_rows, preferred_element_type=jnp.float32)
    latent_part = jnp.concatenate(
        [latent_part[:, :rank_width] + value_part, latent_part[:, rank_width:]], axis=1
    )
    return (query_grad.reshape(count, head_count, width), latent_part)


def shards_by_collectives(queries, latents, out_grad, first_key):
    block_len = queries.shape[0]
    head_local = queries.shape[1]
    width = queries.shape[2]
    rank_width = out_grad.shape[2]
    group_index = lax.axis_index("grp")
    own_block = lax.all_gather(latents, "blk", axis=0, tiled=True)
    prev_block = shifted(own_block, "grp", 1)
    key_rows = jnp.concatenate([prev_block, own_block], axis=0)
    key_iota = jnp.arange(2 * block_len, dtype=jnp.int32)
    key_pos = key_iota + (group_index - 1) * block_len
    in_prev = key_iota < block_len
    piece = min(512, block_len)
    pieces = block_len // piece
    query_steps = queries.reshape(pieces, piece, head_local, width)
    grad_steps = out_grad.reshape(pieces, piece, head_local, rank_width)
    first_steps = first_key.reshape(pieces, piece)
    pos_steps = (jnp.arange(block_len, dtype=jnp.int32) + group_index * block_len).reshape(
        pieces, piece
    )

    def scan_step(carry, items):
        query_blk, grad_blk, first_blk, pos_blk = items
        prev_ok = (key_pos[None, :] >= first_blk[:, None]) & (group_index > 0)
        own_ok = key_pos[None, :] <= pos_blk[:, None]
        visible = jnp.where(in_prev[None, :], prev_ok, own_ok)
        query_part, latent_part = attend_grads(query_blk, grad_blk, key_rows, visible)
        return (carry + latent_part, query_part)

    carry_init = jnp.zeros((2 * block_len, width), jnp.float32)
    latent_part, query_blocks = lax.scan(
        scan_step, carry_init, (query_steps, grad_steps, first_steps, pos_steps)
    )
    query_grad = query_blocks.reshape(block_len, head_local, width)
    prev_part = latent_part[:block_len]
    own_part = latent_part[block_len:]
    from_later = shifted(prev_part.astype(jnp.bfloat16), "grp", -1).astype(prev_part.dtype)
    latent_total = lax.psum_scatter(own_part + from_later, "blk", scatter_dimension=0, tiled=True)
    return (query_grad, latent_total.astype(jnp.bfloat16))


MESH = pl.DeviceIdType.MESH
TILE = 128
HIDDEN = -1e30


def xor(a, b, count):
    out, bit = 0, 1
    while bit < count:
        out = out + bit * ((a // bit + b // bit) % 2)
        bit *= 2
    return out


def dot_nt(a, b):
    return lax.dot_general(a, b, (((1,), (1,)), ((), ())), preferred_element_type=jnp.float32)


def dot_tn(a, b):
    return lax.dot_general(a, b, (((0,), (0,)), ((), ())), preferred_element_type=jnp.float32)


def dot_nn(a, b):
    return jnp.dot(a, b, preferred_element_type=jnp.float32)


def kernel(
    groups, count, q_hbm, lat_hbm, grad_hbm, first_ref, dq_hbm, dl_ref,
    q, grad, kv, s, dp, p, ds, dq, acc, own_acc, part, red, prev_part, next_part,
    in_sem, gat_send, gat_recv, fwd_send, fwd_recv, pp_send, pp_recv, red_send, red_recv, out_sem,
):
    width, block = q.shape
    rank = grad.shape[1]
    rows = block // count
    tiles = block // TILE
    per_tile = TILE // rows
    me = lax.axis_index("blk")
    group = lax.axis_index("grp")
    has_prev = group > 0
    has_next = group < groups - 1
    my_tile = me // per_tile
    prev_tiles = tiles * jnp.minimum(group, 1)

    barrier = pltpu.get_barrier_semaphore()
    for d in range(1, count):
        pl.semaphore_signal(barrier, inc=1, device_id={"blk": xor(me, d, count)}, device_id_type=MESH)

    @pl.when(has_prev)
    def _():
        pl.semaphore_signal(barrier, inc=1, device_id={"grp": group - 1}, device_id_type=MESH)

    @pl.when(has_next)
    def _():
        pl.semaphore_signal(barrier, inc=1, device_id={"grp": group + 1}, device_id_type=MESH)

    own_shard = pltpu.make_async_copy(lat_hbm, kv.at[pl.ds(block + me * rows, rows)], in_sem.at[0])
    q_copy = pltpu.make_async_copy(q_hbm, q, in_sem.at[1])
    grad_copy = pltpu.make_async_copy(grad_hbm, grad, in_sem.at[2])
    own_shard.start()
    q_copy.start()
    grad_copy.start()

    if groups == 2:
        pl.semaphore_wait(barrier, count)
    else:
        ends = jnp.minimum(group, 1) + jnp.minimum(groups - 1 - group, 1)
        pl.semaphore_wait(barrier, count - 1 + ends)

    def gather(d, source, target):
        return pltpu.make_async_remote_copy(
            src_ref=lat_hbm,
            dst_ref=kv.at[pl.ds(block + source * rows, rows)],
            send_sem=gat_send.at[d],
            recv_sem=gat_recv.at[source],
            device_id={"blk": target},
            device_id_type=MESH,
        )

    def forward(j, to):
        return pltpu.make_async_remote_copy(
            src_ref=kv.at[pl.ds(block + j * rows, rows)],
            dst_ref=kv.at[pl.ds(j * rows, rows)],
            send_sem=fwd_send.at[j],
            recv_sem=fwd_recv.at[j],
            device_id={"grp": to},
            device_id_type=MESH,
        )

    def prev_terms(tile, to):
        return pltpu.make_async_remote_copy(
            src_ref=prev_part.at[pl.ds(tile * TILE, TILE)],
            dst_ref=next_part.at[pl.ds(tile * TILE, TILE)],
            send_sem=pp_send.at[tile],
            recv_sem=pp_recv.at[tile],
            device_id={"grp": to},
            device_id_type=MESH,
        )

    def reduce(source, target):
        return pltpu.make_async_remote_copy(
            src_ref=part.at[pl.ds(target * rows, rows)],
            dst_ref=red.at[source],
            send_sem=red_send.at[target],
            recv_sem=red_recv.at[source],
            device_id={"blk": target},
            device_id_type=MESH,
        )

    for d in range(count - 1, 0, -1):
        gather(d, me, xor(me, d, count)).start()
    own_shard.wait()
    q_copy.wait()
    grad_copy.wait()

    key_in_tile = lax.broadcasted_iota(jnp.int32, (TILE, block), 0)
    token = lax.broadcasted_iota(jnp.int32, (TILE, block), 1)

    def scores_of(start, visible, largest):
        at = pl.ds(pl.multiple_of(start, TILE), TILE)
        keys = kv[at, :]
        tile_s = jnp.where(visible, dot_nn(keys, q[...]) * score_scale, HIDDEN)
        s[at, :] = tile_s
        dp[at, :] = dot_nt(keys[:, :rank], grad[...])
        return jnp.maximum(largest, jnp.max(tile_s, axis=0, keepdims=True))

    def own_scores(step, largest):
        tile = xor(my_tile, step, tiles)
        for sub in range(per_tile):
            j = tile * per_tile + sub

            @pl.when(j != me)
            def _():
                gather(0, j, j).wait_recv()

            @pl.when(has_next)
            def _():
                forward(j, group + 1).start()

        return scores_of(block + tile * TILE, tile * TILE + key_in_tile <= token, largest)

    def prev_scores(step, largest):
        tile = xor(my_tile, step, tiles)
        for sub in range(per_tile):
            forward(tile * per_tile + sub, group - 1).wait_recv()
        position = (group - 1) * block + tile * TILE + key_in_tile
        return scores_of(tile * TILE, position >= first_ref[...], largest)

    largest = jnp.full((1, block), HIDDEN, jnp.float32)
    largest = lax.fori_loop(0, tiles, own_scores, largest)
    largest = lax.fori_loop(0, prev_tiles, prev_scores, largest)

    def tile_rows(i):
        return pl.ds(pl.multiple_of(i * TILE, TILE), TILE)

    def exps(i, total):
        at = tile_rows(i)
        e = jnp.exp(s[at, :] - largest)
        s[at, :] = e
        return total + jnp.sum(e, axis=0, keepdims=True)

    zero = jnp.zeros((1, block), jnp.float32)
    first_tile = tiles - prev_tiles
    inverse = 1.0 / lax.fori_loop(first_tile, 2 * tiles, exps, zero)

    def probs(i, delta):
        at = tile_rows(i)
        tile_p = (s[at, :] * inverse).astype(jnp.bfloat16)
        p[at, :] = tile_p
        return delta + jnp.sum(tile_p.astype(jnp.float32) * dp[at, :], axis=0, keepdims=True)

    delta = lax.fori_loop(first_tile, 2 * tiles, probs, zero)

    def score_grads(i, carry):
        at = tile_rows(i)
        ds[at, :] = (p[at, :].astype(jnp.float32) * (dp[at, :] - delta) * score_scale).astype(jnp.bfloat16)
        return carry

    lax.fori_loop(first_tile, 2 * tiles, score_grads, 0)

    def latent_terms(start):
        at = pl.ds(pl.multiple_of(start, TILE), TILE)
        d = ds[at, :]
        acc[...] = dot_nt(d, q[...])
        acc[:, :rank] += dot_nn(p[at, :], grad[...])

    def prev_latents(step, carry):
        tile = xor(my_tile, tiles - 1 - step, tiles)
        latent_terms(tile * TILE)
        prev_part[pl.ds(pl.multiple_of(tile * TILE, TILE), TILE), :] = acc[...].astype(jnp.bfloat16)
        prev_terms(tile, group - 1).start()
        return carry

    lax.fori_loop(0, prev_tiles, prev_latents, 0)

    def query_grads():
        for start in range(0, block, 256):
            cut = slice(start, min(start + 256, block))

            @pl.when(has_prev)
            def _():
                dq[:, cut] = dot_tn(kv[...], ds[:, cut]).astype(jnp.bfloat16)

            @pl.when(group == 0)
            def _():
                dq[:, cut] = dot_tn(kv[block:, :], ds[block:, cut]).astype(jnp.bfloat16)

        pltpu.make_async_copy(dq, dq_hbm, out_sem).start()

    @pl.when(has_next)
    def _():
        query_grads()

    def own_latents(step, carry):
        tile = xor(my_tile, tiles - 1 - step, tiles)
        at = pl.ds(pl.multiple_of(tile * TILE, TILE), TILE)
        latent_terms(block + tile * TILE)

        @pl.when(has_next)
        def _():
            prev_terms(tile, group + 1).wait_recv()
            acc[...] += next_part[at, :].astype(jnp.float32)

        part[at, :] = acc[...].astype(jnp.bfloat16)
        for sub in range(per_tile):
            j = tile * per_tile + sub

            @pl.when(j != me)
            def _():
                reduce(me, j).start()

            @pl.when(j == me)
            def _():
                own_acc[...] = acc[sub * rows:(sub + 1) * rows, :]

        return carry

    lax.fori_loop(0, tiles, own_latents, 0)

    @pl.when(group == groups - 1)
    def _():
        query_grads()

    total = own_acc[...]
    for d in range(1, count):
        source = xor(me, d, count)
        reduce(source, me).wait_recv()
        total = total + red[source].astype(jnp.float32)
    dl_ref[...] = total.astype(dl_ref.dtype)

    pltpu.make_async_copy(dq, dq_hbm, out_sem).wait()
    for d in range(1, count):
        gather(d, me, xor(me, d, count)).wait_send()
        reduce(me, xor(me, d, count)).wait_send()

    @pl.when(has_next)
    def _():
        for j in range(count):
            forward(j, group + 1).wait_send()

    @pl.when(has_prev)
    def _():
        for tile in range(tiles):
            prev_terms(tile, group - 1).wait_send()


def fits(count, block, head_local):
    rows = block // count
    tiles = block // TILE
    powers = count & (count - 1) == 0 and tiles & (tiles - 1) == 0
    return head_local == 1 and rows % 16 == 0 and TILE % rows == 0 and block % TILE == 0 and powers


def shards(queries, latents, out_grad, first_key):
    block, head_local, width = queries.shape
    rank = out_grad.shape[2]
    count, groups = lax.axis_size("blk"), lax.axis_size("grp")
    if not fits(count, block, head_local):
        return shards_by_collectives(queries, latents, out_grad, first_key)
    rows, tiles = block // count, block // TILE
    bf16, f32 = jnp.bfloat16, jnp.float32
    dma = pltpu.SemaphoreType.DMA
    anywhere = pl.BlockSpec(memory_space=pl.ANY)
    vmem = pl.BlockSpec(memory_space=pltpu.VMEM)
    query_grad, latent_grad = pl.pallas_call(
        functools.partial(kernel, groups, count),
        out_shape=(
            jax.ShapeDtypeStruct((width, block), bf16),
            jax.ShapeDtypeStruct((rows, width), bf16),
        ),
        in_specs=[anywhere, anywhere, anywhere, vmem],
        out_specs=(anywhere, vmem),
        scratch_shapes=[
            pltpu.VMEM((width, block), bf16),
            pltpu.VMEM((block, rank), bf16),
            pltpu.VMEM((2 * block, width), bf16),
            pltpu.VMEM((2 * block, block), f32),
            pltpu.VMEM((2 * block, block), f32),
            pltpu.VMEM((2 * block, block), bf16),
            pltpu.VMEM((2 * block, block), bf16),
            pltpu.VMEM((width, block), bf16),
            pltpu.VMEM((TILE, width), f32),
            pltpu.VMEM((rows, width), f32),
            pltpu.VMEM((block, width), bf16),
            pltpu.VMEM((count, rows, width), bf16),
            pltpu.VMEM((block, width), bf16),
            pltpu.VMEM((block, width), bf16),
            dma((3,)),
            dma((count,)),
            dma((count,)),
            dma((count,)),
            dma((count,)),
            dma((tiles,)),
            dma((tiles,)),
            dma((count,)),
            dma((count,)),
            dma,
        ],
        compiler_params=pltpu.CompilerParams(
            collective_id=0, has_side_effects=True, vmem_limit_bytes=40 * 1024 * 1024
        ),
    )(
        queries.reshape(block, width).T,
        latents,
        out_grad.reshape(block, rank),
        first_key.reshape(1, block),
    )
    return (query_grad.T.reshape(block, 1, width), latent_grad)


def solution(mesh):
    placed = (
        P(("rep", "grp"), "blk", None),
        P(("rep", "grp", "blk"), None),
        P(("rep", "grp"), "blk", None),
        P(("rep", "grp")),
    )
    return jax.shard_map(
        shards,
        mesh=mesh,
        in_specs=placed,
        out_specs=(P(("rep", "grp"), "blk", None), P(("rep", "grp", "blk"), None)),
        check_vma=False,
    )
```

```python
import functools

import jax
import jax.numpy as jnp
from jax import lax
from jax.experimental import pallas as pl
from jax.experimental.pallas import tpu as pltpu
from jax.sharding import PartitionSpec as P

score_scale = 192.0 ** (-0.5)


def shifted(shard, axis, by):
    count = lax.axis_size(axis)
    pairs = [(i, i + by) for i in range(count) if 0 <= i + by < count]
    return lax.ppermute(shard, axis, pairs)


def attend_grads(query_blk, grad_blk, key_rows, visible):
    count, head_count, width = query_blk.shape
    query_rows = query_blk.reshape(count * head_count, width)
    grad_rows = grad_blk.reshape(count * head_count, -1)
    rank_width = grad_rows.shape[1]
    value_rows = key_rows[:, :rank_width]
    scores = jnp.dot(query_rows, key_rows.T, preferred_element_type=jnp.float32) * score_scale
    scores = scores.reshape(count, head_count, -1)
    mask_three = visible[:, None, :]
    row_max = jnp.max(jnp.where(mask_three, scores, -jnp.inf), axis=-1, keepdims=True)
    total = jnp.sum(jnp.where(mask_three, jnp.exp(scores - row_max), 0.0), axis=-1, keepdims=True)
    log_norm = row_max + jnp.log(total)
    attn_probs = jnp.where(mask_three, jnp.exp(scores - log_norm), 0.0).astype(jnp.bfloat16)
    attn_probs = attn_probs.reshape(count * head_count, -1)
    outputs = jnp.dot(attn_probs, value_rows, preferred_element_type=jnp.float32)
    row_delta = jnp.sum(grad_rows.astype(jnp.float32) * outputs, axis=-1, keepdims=True)
    prob_grad = jnp.dot(grad_rows, value_rows.T, preferred_element_type=jnp.float32)
    score_grad = (attn_probs.astype(jnp.float32) * (prob_grad - row_delta) * score_scale).astype(
        jnp.bfloat16
    )
    query_grad = jnp.dot(score_grad, key_rows, preferred_element_type=jnp.float32).astype(
        jnp.bfloat16
    )
    latent_part = jnp.dot(score_grad.T, query_rows, preferred_element_type=jnp.float32)
    value_part = jnp.dot(attn_probs.T, grad_rows, preferred_element_type=jnp.float32)
    latent_part = jnp.concatenate(
        [latent_part[:, :rank_width] + value_part, latent_part[:, rank_width:]], axis=1
    )
    return (query_grad.reshape(count, head_count, width), latent_part)


def shards_by_collectives(queries, latents, out_grad, first_key):
    block_len = queries.shape[0]
    head_local = queries.shape[1]
    width = queries.shape[2]
    rank_width = out_grad.shape[2]
    group_index = lax.axis_index("grp")
    own_block = lax.all_gather(latents, "blk", axis=0, tiled=True)
    prev_block = shifted(own_block, "grp", 1)
    key_rows = jnp.concatenate([prev_block, own_block], axis=0)
    key_iota = jnp.arange(2 * block_len, dtype=jnp.int32)
    key_pos = key_iota + (group_index - 1) * block_len
    in_prev = key_iota < block_len
    piece = min(512, block_len)
    pieces = block_len // piece
    query_steps = queries.reshape(pieces, piece, head_local, width)
    grad_steps = out_grad.reshape(pieces, piece, head_local, rank_width)
    first_steps = first_key.reshape(pieces, piece)
    pos_steps = (jnp.arange(block_len, dtype=jnp.int32) + group_index * block_len).reshape(
        pieces, piece
    )

    def scan_step(carry, items):
        query_blk, grad_blk, first_blk, pos_blk = items
        prev_ok = (key_pos[None, :] >= first_blk[:, None]) & (group_index > 0)
        own_ok = key_pos[None, :] <= pos_blk[:, None]
        visible = jnp.where(in_prev[None, :], prev_ok, own_ok)
        query_part, latent_part = attend_grads(query_blk, grad_blk, key_rows, visible)
        return (carry + latent_part, query_part)

    carry_init = jnp.zeros((2 * block_len, width), jnp.float32)
    latent_part, query_blocks = lax.scan(
        scan_step, carry_init, (query_steps, grad_steps, first_steps, pos_steps)
    )
    query_grad = query_blocks.reshape(block_len, head_local, width)
    prev_part = latent_part[:block_len]
    own_part = latent_part[block_len:]
    from_later = shifted(prev_part.astype(jnp.bfloat16), "grp", -1).astype(prev_part.dtype)
    latent_total = lax.psum_scatter(own_part + from_later, "blk", scatter_dimension=0, tiled=True)
    return (query_grad, latent_total.astype(jnp.bfloat16))


MESH = pl.DeviceIdType.MESH
TILE = 128
HIDDEN = -1e30


def xor(a, b, count):
    out, bit = 0, 1
    while bit < count:
        out = out + bit * ((a // bit + b // bit) % 2)
        bit *= 2
    return out


def dot_nt(a, b):
    return lax.dot_general(a, b, (((1,), (1,)), ((), ())), preferred_element_type=jnp.float32)


def dot_tn(a, b):
    return lax.dot_general(a, b, (((0,), (0,)), ((), ())), preferred_element_type=jnp.float32)


def dot_nn(a, b):
    return jnp.dot(a, b, preferred_element_type=jnp.float32)


def kernel(
    groups, count, q_hbm, lat_hbm, grad_hbm, first_ref, dq_hbm, dl_ref,
    q, grad, kv, s, dp, p, ds, dq, acc, keep, pair_part, pair_in, part, red, prev_part, next_part,
    in_sem, gat_send, hop_send, gat_recv, fwd_send, fwd_recv, pp_send, pp_recv,
    pair_send, pair_recv, red_send, red_recv, out_sem,
):
    width, block = q.shape
    rank = grad.shape[1]
    rows = block // count
    tiles = block // TILE
    me = lax.axis_index("blk")
    group = lax.axis_index("grp")
    has_prev = group > 0
    has_next = group < groups - 1
    my_tile, side = me // 2, me % 2
    neighbour = my_tile * 2 + 1 - side
    prev_tiles = tiles * jnp.minimum(group, 1)

    own_shard = pltpu.make_async_copy(lat_hbm, kv.at[pl.ds(block + me * rows, rows)], in_sem.at[0])
    q_copy = pltpu.make_async_copy(q_hbm, q, in_sem.at[1])
    grad_copy = pltpu.make_async_copy(grad_hbm, grad, in_sem.at[2])
    own_shard.start()
    q_copy.start()
    grad_copy.start()

    def column(d):
        return xor(my_tile, d, tiles) * 2 + side

    barrier = pltpu.get_barrier_semaphore()
    pl.semaphore_signal(barrier, inc=1, device_id={"blk": neighbour}, device_id_type=MESH)
    for d in range(1, tiles):
        pl.semaphore_signal(barrier, inc=1, device_id={"blk": column(d)}, device_id_type=MESH)

    @pl.when(has_prev)
    def _():
        pl.semaphore_signal(barrier, inc=1, device_id={"grp": group - 1}, device_id_type=MESH)

    @pl.when(has_next)
    def _():
        pl.semaphore_signal(barrier, inc=1, device_id={"grp": group + 1}, device_id_type=MESH)

    own_shard.wait()
    if groups == 2:
        pl.semaphore_wait(barrier, tiles + 1)
    else:
        ends = jnp.minimum(group, 1) + jnp.minimum(groups - 1 - group, 1)
        pl.semaphore_wait(barrier, tiles + ends)

    def shard(j):
        return kv.at[pl.ds(block + j * rows, rows)]

    def spread(d, source, target):
        return pltpu.make_async_remote_copy(
            src_ref=shard(source),
            dst_ref=shard(source),
            send_sem=gat_send.at[d],
            recv_sem=gat_recv.at[source],
            device_id={"blk": target},
            device_id_type=MESH,
        )

    def hop(tile, j):
        return pltpu.make_async_remote_copy(
            src_ref=shard(j),
            dst_ref=shard(j),
            send_sem=hop_send.at[tile],
            recv_sem=gat_recv.at[j],
            device_id={"blk": neighbour},
            device_id_type=MESH,
        )

    def forward(j, to):
        return pltpu.make_async_remote_copy(
            src_ref=kv.at[pl.ds(block + j * rows, rows)],
            dst_ref=kv.at[pl.ds(j * rows, rows)],
            send_sem=fwd_send.at[j],
            recv_sem=fwd_recv.at[j],
            device_id={"grp": to},
            device_id_type=MESH,
        )

    def prev_terms(tile, to):
        return pltpu.make_async_remote_copy(
            src_ref=prev_part.at[pl.ds(tile * TILE, TILE)],
            dst_ref=next_part.at[pl.ds(tile * TILE, TILE)],
            send_sem=pp_send.at[tile],
            recv_sem=pp_recv.at[tile],
            device_id={"grp": to},
            device_id_type=MESH,
        )

    def pair(tile):
        return pltpu.make_async_remote_copy(
            src_ref=pair_part.at[tile],
            dst_ref=pair_in.at[tile],
            send_sem=pair_send.at[tile],
            recv_sem=pair_recv.at[tile],
            device_id={"blk": neighbour},
            device_id_type=MESH,
        )

    def reduce(source, target):
        return pltpu.make_async_remote_copy(
            src_ref=part.at[target],
            dst_ref=red.at[source],
            send_sem=red_send.at[target],
            recv_sem=red_recv.at[source],
            device_id={"blk": target * 2 + side},
            device_id_type=MESH,
        )

    hop(my_tile, me).start()
    for d in range(1, tiles):
        spread(d, me, column(d)).start()

    @pl.when(has_next)
    def _():
        forward(me, group + 1).start()

    q_copy.wait()
    grad_copy.wait()

    key_in_tile = lax.broadcasted_iota(jnp.int32, (TILE, block), 0)
    token = lax.broadcasted_iota(jnp.int32, (TILE, block), 1)

    def scores_of(start, visible, largest):
        at = pl.ds(pl.multiple_of(start, TILE), TILE)
        keys = kv[at, :]
        tile_s = jnp.where(visible, dot_nn(keys, q[...]) * score_scale, HIDDEN)
        s[at, :] = tile_s
        dp[at, :] = dot_nt(keys[:, :rank], grad[...])
        return jnp.maximum(largest, jnp.max(tile_s, axis=0, keepdims=True))

    def relay(step):
        tile = xor(my_tile, step, tiles)
        j = tile * 2 + side
        spread(0, j, j).wait_recv()
        hop(tile, j).start()

        @pl.when(has_next)
        def _():
            forward(j, group + 1).start()

    def own_scores(step, largest):
        @pl.when(step + 1 < tiles)
        def _():
            relay(step + 1)

        tile = xor(my_tile, step, tiles)
        j = tile * 2 + 1 - side
        hop(tile, j).wait_recv()

        @pl.when(has_next)
        def _():
            forward(j, group + 1).start()

        return scores_of(block + tile * TILE, tile * TILE + key_in_tile <= token, largest)

    def prev_scores(step, largest):
        tile = xor(my_tile, step, tiles)
        for j in (tile * 2, tile * 2 + 1):
            forward(j, group - 1).wait_recv()
        position = (group - 1) * block + tile * TILE + key_in_tile
        return scores_of(tile * TILE, position >= first_ref[...], largest)

    largest = jnp.full((1, block), HIDDEN, jnp.float32)
    largest = lax.fori_loop(0, tiles, own_scores, largest)
    largest = lax.fori_loop(0, prev_tiles, prev_scores, largest)

    def tile_rows(i):
        return pl.ds(pl.multiple_of(i * TILE, TILE), TILE)

    def exps(i, total):
        at = tile_rows(i)
        e = jnp.exp(s[at, :] - largest)
        s[at, :] = e
        return total + jnp.sum(e, axis=0, keepdims=True)

    zero = jnp.zeros((1, block), jnp.float32)
    first_tile = tiles - prev_tiles
    inverse = 1.0 / lax.fori_loop(first_tile, 2 * tiles, exps, zero)

    def probs(i, delta):
        at = tile_rows(i)
        tile_p = (s[at, :] * inverse).astype(jnp.bfloat16)
        p[at, :] = tile_p
        return delta + jnp.sum(tile_p.astype(jnp.float32) * dp[at, :], axis=0, keepdims=True)

    delta = lax.fori_loop(first_tile, 2 * tiles, probs, zero)

    def score_grads(i, carry):
        at = tile_rows(i)
        ds[at, :] = (p[at, :].astype(jnp.float32) * (dp[at, :] - delta) * score_scale).astype(jnp.bfloat16)
        return carry

    lax.fori_loop(first_tile, 2 * tiles, score_grads, 0)

    def latent_terms(start):
        at = pl.ds(pl.multiple_of(start, TILE), TILE)
        d = ds[at, :]
        acc[...] = dot_nt(d, q[...])
        acc[:, :rank] += dot_nn(p[at, :], grad[...])

    def prev_latents(step, carry):
        tile = xor(my_tile, tiles - 1 - step, tiles)
        latent_terms(tile * TILE)
        prev_part[pl.ds(pl.multiple_of(tile * TILE, TILE), TILE), :] = acc[...].astype(jnp.bfloat16)
        prev_terms(tile, group - 1).start()
        return carry

    lax.fori_loop(0, prev_tiles, prev_latents, 0)

    def query_grads():
        for start in range(0, block, 256):
            cut = slice(start, min(start + 256, block))

            @pl.when(has_prev)
            def _():
                dq[:, cut] = dot_tn(kv[...], ds[:, cut]).astype(jnp.bfloat16)

            @pl.when(group == 0)
            def _():
                dq[:, cut] = dot_tn(kv[block:, :], ds[block:, cut]).astype(jnp.bfloat16)

        pltpu.make_async_copy(dq, dq_hbm, out_sem).start()

    @pl.when(has_next)
    def _():
        query_grads()

    def pair_sum(step):
        tile = xor(my_tile, step, tiles)
        pair(tile).wait_recv()
        keep[tile] += pair_in[tile].astype(jnp.float32)

        @pl.when(tile != my_tile)
        def _():
            part[tile] = keep[tile].astype(jnp.bfloat16)
            reduce(my_tile, tile).start()

    def own_latents(i, carry):
        step = tiles - 1 - i
        tile = xor(my_tile, step, tiles)
        at = pl.ds(pl.multiple_of(tile * TILE, TILE), TILE)
        latent_terms(block + tile * TILE)

        @pl.when(has_next)
        def _():
            prev_terms(tile, group + 1).wait_recv()
            acc[...] += next_part[at, :].astype(jnp.float32)

        theirs = pl.ds(pl.multiple_of((1 - side) * rows, rows), rows)
        mine = pl.ds(pl.multiple_of(side * rows, rows), rows)
        pair_part[tile] = acc[theirs, :].astype(jnp.bfloat16)
        pair(tile).start()
        keep[tile] = acc[mine, :]

        @pl.when(i > 0)
        def _():
            pair_sum(step + 1)

        return carry

    lax.fori_loop(0, tiles, own_latents, 0)

    @pl.when(group == groups - 1)
    def _():
        query_grads()

    pair_sum(0)
    total = keep[my_tile]
    for d in range(1, tiles):
        source = xor(my_tile, d, tiles)
        reduce(source, my_tile).wait_recv()
        total = total + red[source].astype(jnp.float32)
    dl_ref[...] = total.astype(dl_ref.dtype)

    pltpu.make_async_copy(dq, dq_hbm, out_sem).wait()
    for tile in range(tiles):
        hop(tile, tile * 2 + side).wait_send()
        pair(tile).wait_send()
    for d in range(1, tiles):
        spread(d, me, column(d)).wait_send()
        reduce(my_tile, xor(my_tile, d, tiles)).wait_send()

    @pl.when(has_next)
    def _():
        for j in range(count):
            forward(j, group + 1).wait_send()

    @pl.when(has_prev)
    def _():
        for tile in range(tiles):
            prev_terms(tile, group - 1).wait_send()


def fits(count, block, head_local):
    rows = block // count
    tiles = block // TILE
    powers = count & (count - 1) == 0 and tiles & (tiles - 1) == 0
    return head_local == 1 and rows % 16 == 0 and TILE == 2 * rows and block % TILE == 0 and powers


def shards(queries, latents, out_grad, first_key):
    block, head_local, width = queries.shape
    rank = out_grad.shape[2]
    count, groups = lax.axis_size("blk"), lax.axis_size("grp")
    if not fits(count, block, head_local):
        return shards_by_collectives(queries, latents, out_grad, first_key)
    rows, tiles = block // count, block // TILE
    bf16, f32 = jnp.bfloat16, jnp.float32
    dma = pltpu.SemaphoreType.DMA
    anywhere = pl.BlockSpec(memory_space=pltpu.HBM)
    vmem = pl.BlockSpec(memory_space=pltpu.VMEM)
    query_grad, latent_grad = pl.pallas_call(
        functools.partial(kernel, groups, count),
        out_shape=(
            jax.ShapeDtypeStruct((width, block), bf16),
            jax.ShapeDtypeStruct((rows, width), bf16),
        ),
        in_specs=[anywhere, anywhere, anywhere, vmem],
        out_specs=(anywhere, vmem),
        scratch_shapes=[
            pltpu.VMEM((width, block), bf16),
            pltpu.VMEM((block, rank), bf16),
            pltpu.VMEM((2 * block, width), bf16),
            pltpu.VMEM((2 * block, block), f32),
            pltpu.VMEM((2 * block, block), f32),
            pltpu.VMEM((2 * block, block), bf16),
            pltpu.VMEM((2 * block, block), bf16),
            pltpu.VMEM((width, block), bf16),
            pltpu.VMEM((TILE, width), f32),
            pltpu.VMEM((tiles, rows, width), f32),
            pltpu.VMEM((tiles, rows, width), bf16),
            pltpu.VMEM((tiles, rows, width), bf16),
            pltpu.VMEM((tiles, rows, width), bf16),
            pltpu.VMEM((tiles, rows, width), bf16),
            pltpu.VMEM((block, width), bf16),
            pltpu.VMEM((block, width), bf16),
            dma((3,)),
            dma((tiles,)),
            dma((tiles,)),
            dma((count,)),
            dma((count,)),
            dma((count,)),
            dma((tiles,)),
            dma((tiles,)),
            dma((tiles,)),
            dma((tiles,)),
            dma((tiles,)),
            dma((tiles,)),
            dma,
        ],
        compiler_params=pltpu.CompilerParams(
            collective_id=0, has_side_effects=True, vmem_limit_bytes=63 * 1024 * 1024
        ),
    )(
        queries.reshape(block, width).T,
        latents,
        out_grad.reshape(block, rank),
        first_key.reshape(1, block),
    )
    return (query_grad.T.reshape(block, 1, width), latent_grad)


def solution(mesh):
    placed = (
        P(("rep", "grp"), "blk", None),
        P(("rep", "grp", "blk"), None),
        P(("rep", "grp"), "blk", None),
        P(("rep", "grp")),
    )
    return jax.shard_map(
        shards,
        mesh=mesh,
        in_specs=placed,
        out_specs=(P(("rep", "grp"), "blk", None), P(("rep", "grp", "blk"), None)),
        check_vma=False,
    )
```

```python
import functools

import jax
import jax.numpy as jnp
from jax import lax
from jax.experimental import pallas as pl
from jax.experimental.pallas import tpu as pltpu
from jax.sharding import PartitionSpec as P

score_scale = 192.0 ** (-0.5)


def shifted(shard, axis, by):
    count = lax.axis_size(axis)
    pairs = [(i, i + by) for i in range(count) if 0 <= i + by < count]
    return lax.ppermute(shard, axis, pairs)


def attend_grads(query_blk, grad_blk, key_rows, visible):
    count, head_count, width = query_blk.shape
    query_rows = query_blk.reshape(count * head_count, width)
    grad_rows = grad_blk.reshape(count * head_count, -1)
    rank_width = grad_rows.shape[1]
    value_rows = key_rows[:, :rank_width]
    scores = jnp.dot(query_rows, key_rows.T, preferred_element_type=jnp.float32) * score_scale
    scores = scores.reshape(count, head_count, -1)
    mask_three = visible[:, None, :]
    row_max = jnp.max(jnp.where(mask_three, scores, -jnp.inf), axis=-1, keepdims=True)
    total = jnp.sum(jnp.where(mask_three, jnp.exp(scores - row_max), 0.0), axis=-1, keepdims=True)
    log_norm = row_max + jnp.log(total)
    attn_probs = jnp.where(mask_three, jnp.exp(scores - log_norm), 0.0).astype(jnp.bfloat16)
    attn_probs = attn_probs.reshape(count * head_count, -1)
    outputs = jnp.dot(attn_probs, value_rows, preferred_element_type=jnp.float32)
    row_delta = jnp.sum(grad_rows.astype(jnp.float32) * outputs, axis=-1, keepdims=True)
    prob_grad = jnp.dot(grad_rows, value_rows.T, preferred_element_type=jnp.float32)
    score_grad = (attn_probs.astype(jnp.float32) * (prob_grad - row_delta) * score_scale).astype(
        jnp.bfloat16
    )
    query_grad = jnp.dot(score_grad, key_rows, preferred_element_type=jnp.float32).astype(
        jnp.bfloat16
    )
    latent_part = jnp.dot(score_grad.T, query_rows, preferred_element_type=jnp.float32)
    value_part = jnp.dot(attn_probs.T, grad_rows, preferred_element_type=jnp.float32)
    latent_part = jnp.concatenate(
        [latent_part[:, :rank_width] + value_part, latent_part[:, rank_width:]], axis=1
    )
    return (query_grad.reshape(count, head_count, width), latent_part)


def shards_by_collectives(queries, latents, out_grad, first_key):
    block_len = queries.shape[0]
    head_local = queries.shape[1]
    width = queries.shape[2]
    rank_width = out_grad.shape[2]
    group_index = lax.axis_index("grp")
    own_block = lax.all_gather(latents, "blk", axis=0, tiled=True)
    prev_block = shifted(own_block, "grp", 1)
    key_rows = jnp.concatenate([prev_block, own_block], axis=0)
    key_iota = jnp.arange(2 * block_len, dtype=jnp.int32)
    key_pos = key_iota + (group_index - 1) * block_len
    in_prev = key_iota < block_len
    piece = min(512, block_len)
    pieces = block_len // piece
    query_steps = queries.reshape(pieces, piece, head_local, width)
    grad_steps = out_grad.reshape(pieces, piece, head_local, rank_width)
    first_steps = first_key.reshape(pieces, piece)
    pos_steps = (jnp.arange(block_len, dtype=jnp.int32) + group_index * block_len).reshape(
        pieces, piece
    )

    def scan_step(carry, items):
        query_blk, grad_blk, first_blk, pos_blk = items
        prev_ok = (key_pos[None, :] >= first_blk[:, None]) & (group_index > 0)
        own_ok = key_pos[None, :] <= pos_blk[:, None]
        visible = jnp.where(in_prev[None, :], prev_ok, own_ok)
        query_part, latent_part = attend_grads(query_blk, grad_blk, key_rows, visible)
        return (carry + latent_part, query_part)

    carry_init = jnp.zeros((2 * block_len, width), jnp.float32)
    latent_part, query_blocks = lax.scan(
        scan_step, carry_init, (query_steps, grad_steps, first_steps, pos_steps)
    )
    query_grad = query_blocks.reshape(block_len, head_local, width)
    prev_part = latent_part[:block_len]
    own_part = latent_part[block_len:]
    from_later = shifted(prev_part.astype(jnp.bfloat16), "grp", -1).astype(prev_part.dtype)
    latent_total = lax.psum_scatter(own_part + from_later, "blk", scatter_dimension=0, tiled=True)
    return (query_grad, latent_total.astype(jnp.bfloat16))


MESH = pl.DeviceIdType.MESH
TILE = 128
HIDDEN = -1e30


def xor(a, b, count):
    out, bit = 0, 1
    while bit < count:
        out = out + bit * ((a // bit + b // bit) % 2)
        bit *= 2
    return out


def dot_nt(a, b):
    return lax.dot_general(a, b, (((1,), (1,)), ((), ())), preferred_element_type=jnp.float32)


def dot_tn(a, b):
    return lax.dot_general(a, b, (((0,), (0,)), ((), ())), preferred_element_type=jnp.float32)


def dot_nn(a, b):
    return jnp.dot(a, b, preferred_element_type=jnp.float32)


def kernel(
    groups, count, q_hbm, lat_hbm, grad_hbm, first_ref, dq_hbm, dl_ref,
    q, grad, kv, s, dp, p, ds, dq, tops, sums, acc, keep, pair_part, pair_in, part, red, prev_part, next_part,
    in_sem, gat_send, hop_send, gat_recv, fwd_send, fwd_recv, pp_send, pp_recv,
    pair_send, pair_recv, red_send, red_recv, out_sem,
):
    width, block = q.shape
    rank = grad.shape[1]
    rows = block // count
    tiles = block // TILE
    me = lax.axis_index("blk")
    group = lax.axis_index("grp")
    has_prev = group > 0
    has_next = group < groups - 1
    my_tile, side = me // 2, me % 2
    neighbour = my_tile * 2 + 1 - side
    prev_tiles = tiles * jnp.minimum(group, 1)

    own_shard = pltpu.make_async_copy(lat_hbm, kv.at[pl.ds(block + me * rows, rows)], in_sem.at[0])
    q_copy = pltpu.make_async_copy(q_hbm, q, in_sem.at[1])
    grad_copy = pltpu.make_async_copy(grad_hbm, grad, in_sem.at[2])
    own_shard.start()
    q_copy.start()
    grad_copy.start()

    def column(d):
        return xor(my_tile, d, tiles) * 2 + side

    barrier = pltpu.get_barrier_semaphore()
    pl.semaphore_signal(barrier, inc=1, device_id={"blk": neighbour}, device_id_type=MESH)
    for d in range(1, tiles):
        pl.semaphore_signal(barrier, inc=1, device_id={"blk": column(d)}, device_id_type=MESH)

    @pl.when(has_prev)
    def _():
        pl.semaphore_signal(barrier, inc=1, device_id={"grp": group - 1}, device_id_type=MESH)

    @pl.when(has_next)
    def _():
        pl.semaphore_signal(barrier, inc=1, device_id={"grp": group + 1}, device_id_type=MESH)

    own_shard.wait()
    if groups == 2:
        pl.semaphore_wait(barrier, tiles + 1)
    else:
        ends = jnp.minimum(group, 1) + jnp.minimum(groups - 1 - group, 1)
        pl.semaphore_wait(barrier, tiles + ends)

    def shard(j):
        return kv.at[pl.ds(block + j * rows, rows)]

    def spread(d, source, target):
        return pltpu.make_async_remote_copy(
            src_ref=shard(source),
            dst_ref=shard(source),
            send_sem=gat_send.at[d],
            recv_sem=gat_recv.at[source],
            device_id={"blk": target},
            device_id_type=MESH,
        )

    def hop(tile, j):
        return pltpu.make_async_remote_copy(
            src_ref=shard(j),
            dst_ref=shard(j),
            send_sem=hop_send.at[tile],
            recv_sem=gat_recv.at[j],
            device_id={"blk": neighbour},
            device_id_type=MESH,
        )

    def forward(j, to):
        return pltpu.make_async_remote_copy(
            src_ref=kv.at[pl.ds(block + j * rows, rows)],
            dst_ref=kv.at[pl.ds(j * rows, rows)],
            send_sem=fwd_send.at[j],
            recv_sem=fwd_recv.at[j],
            device_id={"grp": to},
            device_id_type=MESH,
        )

    def prev_terms(tile, to):
        return pltpu.make_async_remote_copy(
            src_ref=prev_part.at[pl.ds(tile * TILE, TILE)],
            dst_ref=next_part.at[pl.ds(tile * TILE, TILE)],
            send_sem=pp_send.at[tile],
            recv_sem=pp_recv.at[tile],
            device_id={"grp": to},
            device_id_type=MESH,
        )

    def pair(tile):
        return pltpu.make_async_remote_copy(
            src_ref=pair_part.at[tile],
            dst_ref=pair_in.at[tile],
            send_sem=pair_send.at[tile],
            recv_sem=pair_recv.at[tile],
            device_id={"blk": neighbour},
            device_id_type=MESH,
        )

    def reduce(source, target):
        return pltpu.make_async_remote_copy(
            src_ref=part.at[target],
            dst_ref=red.at[source],
            send_sem=red_send.at[target],
            recv_sem=red_recv.at[source],
            device_id={"blk": target * 2 + side},
            device_id_type=MESH,
        )

    hop(my_tile, me).start()
    for d in range(1, tiles):
        spread(d, me, column(d)).start()

    @pl.when(has_next)
    def _():
        forward(me, group + 1).start()

    q_copy.wait()
    grad_copy.wait()

    key_in_tile = lax.broadcasted_iota(jnp.int32, (TILE, block), 0)
    token = lax.broadcasted_iota(jnp.int32, (TILE, block), 1)

    def scores_of(start, visible, largest):
        at = pl.ds(pl.multiple_of(start, TILE), TILE)
        keys = kv[at, :]
        tile_s = jnp.where(visible, dot_nn(keys, q[...]) * score_scale, HIDDEN)
        dp[at, :] = dot_nt(keys[:, :rank], grad[...])
        top = jnp.max(tile_s, axis=0, keepdims=True)
        e = jnp.exp(tile_s - top)
        s[at, :] = e
        tops[start // TILE] = top
        sums[start // TILE] = jnp.sum(e, axis=0, keepdims=True)
        return jnp.maximum(largest, top)

    def relay(step):
        tile = xor(my_tile, step, tiles)
        j = tile * 2 + side
        spread(0, j, j).wait_recv()
        hop(tile, j).start()

        @pl.when(has_next)
        def _():
            forward(j, group + 1).start()

    def own_scores(step, largest):
        @pl.when(step + 1 < tiles)
        def _():
            relay(step + 1)

        tile = xor(my_tile, step, tiles)
        j = tile * 2 + 1 - side
        hop(tile, j).wait_recv()

        @pl.when(has_next)
        def _():
            forward(j, group + 1).start()

        return scores_of(block + tile * TILE, tile * TILE + key_in_tile <= token, largest)

    def prev_scores(step, largest):
        tile = xor(my_tile, step, tiles)
        for j in (tile * 2, tile * 2 + 1):
            forward(j, group - 1).wait_recv()
        position = (group - 1) * block + tile * TILE + key_in_tile
        return scores_of(tile * TILE, position >= first_ref[...], largest)

    largest = jnp.full((1, block), HIDDEN, jnp.float32)
    largest = lax.fori_loop(0, tiles, own_scores, largest)
    largest = lax.fori_loop(0, prev_tiles, prev_scores, largest)

    def tile_rows(i):
        return pl.ds(pl.multiple_of(i * TILE, TILE), TILE)

    def rescale(i, total):
        factor = jnp.exp(tops[i] - largest)
        tops[i] = factor
        return total + factor * sums[i]

    zero = jnp.zeros((1, block), jnp.float32)
    first_tile = tiles - prev_tiles
    inverse = 1.0 / lax.fori_loop(first_tile, 2 * tiles, rescale, zero)

    def probs(i, delta):
        at = tile_rows(i)
        tile_p = (s[at, :] * (tops[i] * inverse)).astype(jnp.bfloat16)
        p[at, :] = tile_p
        return delta + jnp.sum(tile_p.astype(jnp.float32) * dp[at, :], axis=0, keepdims=True)

    delta = lax.fori_loop(first_tile, 2 * tiles, probs, zero)

    def score_grads(at):
        tile_d = p[at, :].astype(jnp.float32) * (dp[at, :] - delta) * score_scale
        ds[at, :] = tile_d.astype(jnp.bfloat16)

    def latent_terms(start):
        at = pl.ds(pl.multiple_of(start, TILE), TILE)
        score_grads(at)
        acc[...] = dot_nt(ds[at, :], q[...])
        acc[:, :rank] += dot_nn(p[at, :], grad[...])

    def prev_latents(step, carry):
        tile = xor(my_tile, tiles - 1 - step, tiles)
        latent_terms(tile * TILE)
        prev_part[pl.ds(pl.multiple_of(tile * TILE, TILE), TILE), :] = acc[...].astype(jnp.bfloat16)
        prev_terms(tile, group - 1).start()
        return carry

    lax.fori_loop(0, prev_tiles, prev_latents, 0)

    def query_grads():
        for start in range(0, block, 256):
            cut = slice(start, min(start + 256, block))

            @pl.when(has_prev)
            def _():
                dq[:, cut] = dot_tn(kv[...], ds[:, cut]).astype(jnp.bfloat16)

            @pl.when(group == 0)
            def _():
                dq[:, cut] = dot_tn(kv[block:, :], ds[block:, cut]).astype(jnp.bfloat16)

        pltpu.make_async_copy(dq, dq_hbm, out_sem).start()

    @pl.when(has_next)
    def _():
        for i in range(tiles, 2 * tiles):
            score_grads(pl.ds(i * TILE, TILE))
        query_grads()

    def pair_sum(step):
        tile = xor(my_tile, step, tiles)
        pair(tile).wait_recv()
        keep[tile] += pair_in[tile].astype(jnp.float32)

        @pl.when(tile != my_tile)
        def _():
            part[tile] = keep[tile].astype(jnp.bfloat16)
            reduce(my_tile, tile).start()

    def own_latents(i, carry):
        step = tiles - 1 - i
        tile = xor(my_tile, step, tiles)
        at = pl.ds(pl.multiple_of(tile * TILE, TILE), TILE)
        latent_terms(block + tile * TILE)

        @pl.when(has_next)
        def _():
            prev_terms(tile, group + 1).wait_recv()
            acc[...] += next_part[at, :].astype(jnp.float32)

        theirs = pl.ds(pl.multiple_of((1 - side) * rows, rows), rows)
        mine = pl.ds(pl.multiple_of(side * rows, rows), rows)
        pair_part[tile] = acc[theirs, :].astype(jnp.bfloat16)
        pair(tile).start()
        keep[tile] = acc[mine, :]

        @pl.when(i > 0)
        def _():
            pair_sum(step + 1)

        return carry

    lax.fori_loop(0, tiles, own_latents, 0)

    @pl.when(group == groups - 1)
    def _():
        query_grads()

    pair_sum(0)
    total = keep[my_tile]
    for d in range(1, tiles):
        source = xor(my_tile, d, tiles)
        reduce(source, my_tile).wait_recv()
        total = total + red[source].astype(jnp.float32)
    dl_ref[...] = total.astype(dl_ref.dtype)

    pltpu.make_async_copy(dq, dq_hbm, out_sem).wait()
    for tile in range(tiles):
        hop(tile, tile * 2 + side).wait_send()
        pair(tile).wait_send()
    for d in range(1, tiles):
        spread(d, me, column(d)).wait_send()
        reduce(my_tile, xor(my_tile, d, tiles)).wait_send()

    @pl.when(has_next)
    def _():
        for j in range(count):
            forward(j, group + 1).wait_send()

    @pl.when(has_prev)
    def _():
        for tile in range(tiles):
            prev_terms(tile, group - 1).wait_send()


def fits(count, block, head_local):
    rows = block // count
    tiles = block // TILE
    powers = count & (count - 1) == 0 and tiles & (tiles - 1) == 0
    return head_local == 1 and rows % 16 == 0 and TILE == 2 * rows and block % TILE == 0 and powers


def shards(queries, latents, out_grad, first_key):
    block, head_local, width = queries.shape
    rank = out_grad.shape[2]
    count, groups = lax.axis_size("blk"), lax.axis_size("grp")
    if not fits(count, block, head_local):
        return shards_by_collectives(queries, latents, out_grad, first_key)
    rows, tiles = block // count, block // TILE
    bf16, f32 = jnp.bfloat16, jnp.float32
    dma = pltpu.SemaphoreType.DMA
    anywhere = pl.BlockSpec(memory_space=pltpu.HBM)
    vmem = pl.BlockSpec(memory_space=pltpu.VMEM)
    query_grad, latent_grad = pl.pallas_call(
        functools.partial(kernel, groups, count),
        out_shape=(
            jax.ShapeDtypeStruct((width, block), bf16),
            jax.ShapeDtypeStruct((rows, width), bf16),
        ),
        in_specs=[anywhere, anywhere, anywhere, vmem],
        out_specs=(anywhere, vmem),
        scratch_shapes=[
            pltpu.VMEM((width, block), bf16),
            pltpu.VMEM((block, rank), bf16),
            pltpu.VMEM((2 * block, width), bf16),
            pltpu.VMEM((2 * block, block), f32),
            pltpu.VMEM((2 * block, block), f32),
            pltpu.VMEM((2 * block, block), bf16),
            pltpu.VMEM((2 * block, block), bf16),
            pltpu.VMEM((width, block), bf16),
            pltpu.VMEM((2 * tiles, 1, block), f32),
            pltpu.VMEM((2 * tiles, 1, block), f32),
            pltpu.VMEM((TILE, width), f32),
            pltpu.VMEM((tiles, rows, width), f32),
            pltpu.VMEM((tiles, rows, width), bf16),
            pltpu.VMEM((tiles, rows, width), bf16),
            pltpu.VMEM((tiles, rows, width), bf16),
            pltpu.VMEM((tiles, rows, width), bf16),
            pltpu.VMEM((block, width), bf16),
            pltpu.VMEM((block, width), bf16),
            dma((3,)),
            dma((tiles,)),
            dma((tiles,)),
            dma((count,)),
            dma((count,)),
            dma((count,)),
            dma((tiles,)),
            dma((tiles,)),
            dma((tiles,)),
            dma((tiles,)),
            dma((tiles,)),
            dma((tiles,)),
            dma,
        ],
        compiler_params=pltpu.CompilerParams(
            collective_id=0, has_side_effects=True, vmem_limit_bytes=63 * 1024 * 1024
        ),
    )(
        queries.reshape(block, width).T,
        latents,
        out_grad.reshape(block, rank),
        first_key.reshape(1, block),
    )
    return (query_grad.T.reshape(block, 1, width), latent_grad)


def solution(mesh):
    placed = (
        P(("rep", "grp"), "blk", None),
        P(("rep", "grp", "blk"), None),
        P(("rep", "grp"), "blk", None),
        P(("rep", "grp")),
    )
    return jax.shard_map(
        shards,
        mesh=mesh,
        in_specs=placed,
        out_specs=(P(("rep", "grp"), "blk", None), P(("rep", "grp", "blk"), None)),
        check_vma=False,
    )
```

```python
import functools

import jax
import jax.numpy as jnp
from jax import lax
from jax.experimental import pallas as pl
from jax.experimental.pallas import tpu as pltpu
from jax.sharding import PartitionSpec as P

score_scale = 192.0 ** (-0.5)


def shifted(shard, axis, by):
    count = lax.axis_size(axis)
    pairs = [(i, i + by) for i in range(count) if 0 <= i + by < count]
    return lax.ppermute(shard, axis, pairs)


def attend_grads(query_blk, grad_blk, key_rows, visible):
    count, head_count, width = query_blk.shape
    query_rows = query_blk.reshape(count * head_count, width)
    grad_rows = grad_blk.reshape(count * head_count, -1)
    rank_width = grad_rows.shape[1]
    value_rows = key_rows[:, :rank_width]
    scores = jnp.dot(query_rows, key_rows.T, preferred_element_type=jnp.float32) * score_scale
    scores = scores.reshape(count, head_count, -1)
    mask_three = visible[:, None, :]
    row_max = jnp.max(jnp.where(mask_three, scores, -jnp.inf), axis=-1, keepdims=True)
    total = jnp.sum(jnp.where(mask_three, jnp.exp(scores - row_max), 0.0), axis=-1, keepdims=True)
    log_norm = row_max + jnp.log(total)
    attn_probs = jnp.where(mask_three, jnp.exp(scores - log_norm), 0.0).astype(jnp.bfloat16)
    attn_probs = attn_probs.reshape(count * head_count, -1)
    outputs = jnp.dot(attn_probs, value_rows, preferred_element_type=jnp.float32)
    row_delta = jnp.sum(grad_rows.astype(jnp.float32) * outputs, axis=-1, keepdims=True)
    prob_grad = jnp.dot(grad_rows, value_rows.T, preferred_element_type=jnp.float32)
    score_grad = (attn_probs.astype(jnp.float32) * (prob_grad - row_delta) * score_scale).astype(
        jnp.bfloat16
    )
    query_grad = jnp.dot(score_grad, key_rows, preferred_element_type=jnp.float32).astype(
        jnp.bfloat16
    )
    latent_part = jnp.dot(score_grad.T, query_rows, preferred_element_type=jnp.float32)
    value_part = jnp.dot(attn_probs.T, grad_rows, preferred_element_type=jnp.float32)
    latent_part = jnp.concatenate(
        [latent_part[:, :rank_width] + value_part, latent_part[:, rank_width:]], axis=1
    )
    return (query_grad.reshape(count, head_count, width), latent_part)


def shards_by_collectives(queries, latents, out_grad, first_key):
    block_len = queries.shape[0]
    head_local = queries.shape[1]
    width = queries.shape[2]
    rank_width = out_grad.shape[2]
    group_index = lax.axis_index("grp")
    own_block = lax.all_gather(latents, "blk", axis=0, tiled=True)
    prev_block = shifted(own_block, "grp", 1)
    key_rows = jnp.concatenate([prev_block, own_block], axis=0)
    key_iota = jnp.arange(2 * block_len, dtype=jnp.int32)
    key_pos = key_iota + (group_index - 1) * block_len
    in_prev = key_iota < block_len
    piece = min(512, block_len)
    pieces = block_len // piece
    query_steps = queries.reshape(pieces, piece, head_local, width)
    grad_steps = out_grad.reshape(pieces, piece, head_local, rank_width)
    first_steps = first_key.reshape(pieces, piece)
    pos_steps = (jnp.arange(block_len, dtype=jnp.int32) + group_index * block_len).reshape(
        pieces, piece
    )

    def scan_step(carry, items):
        query_blk, grad_blk, first_blk, pos_blk = items
        prev_ok = (key_pos[None, :] >= first_blk[:, None]) & (group_index > 0)
        own_ok = key_pos[None, :] <= pos_blk[:, None]
        visible = jnp.where(in_prev[None, :], prev_ok, own_ok)
        query_part, latent_part = attend_grads(query_blk, grad_blk, key_rows, visible)
        return (carry + latent_part, query_part)

    carry_init = jnp.zeros((2 * block_len, width), jnp.float32)
    latent_part, query_blocks = lax.scan(
        scan_step, carry_init, (query_steps, grad_steps, first_steps, pos_steps)
    )
    query_grad = query_blocks.reshape(block_len, head_local, width)
    prev_part = latent_part[:block_len]
    own_part = latent_part[block_len:]
    from_later = shifted(prev_part.astype(jnp.bfloat16), "grp", -1).astype(prev_part.dtype)
    latent_total = lax.psum_scatter(own_part + from_later, "blk", scatter_dimension=0, tiled=True)
    return (query_grad, latent_total.astype(jnp.bfloat16))


MESH = pl.DeviceIdType.MESH
TILE = 128
HIDDEN = -1e30


def xor(a, b, count):
    out, bit = 0, 1
    while bit < count:
        out = out + bit * ((a // bit + b // bit) % 2)
        bit *= 2
    return out


def dot_nt(a, b):
    return lax.dot_general(a, b, (((1,), (1,)), ((), ())), preferred_element_type=jnp.float32)


def dot_tn(a, b):
    return lax.dot_general(a, b, (((0,), (0,)), ((), ())), preferred_element_type=jnp.float32)


def dot_nn(a, b):
    return jnp.dot(a, b, preferred_element_type=jnp.float32)


def kernel(
    groups, count, q_hbm, lat_hbm, grad_hbm, first_ref, dq_hbm, dl_ref,
    q, grad, kv, s, dp, p, ds, dq, tops, sums, acc, keep, pair_part, pair_in, part, red, prev_part, next_part,
    in_sem, gat_send, hop_send, gat_recv, fwd_send, fwd_recv, pp_send, pp_recv,
    pair_send, pair_recv, red_send, red_recv, out_sem,
):
    width, block = q.shape
    rank = grad.shape[1]
    rows = block // count
    tiles = block // TILE
    me = lax.axis_index("blk")
    group = lax.axis_index("grp")
    has_prev = group > 0
    has_next = group < groups - 1
    my_tile, side = me // 2, me % 2
    neighbour = my_tile * 2 + 1 - side
    prev_tiles = tiles * jnp.minimum(group, 1)

    own_shard = pltpu.make_async_copy(lat_hbm, kv.at[pl.ds(block + me * rows, rows)], in_sem.at[0])
    q_copy = pltpu.make_async_copy(q_hbm, q, in_sem.at[1])
    grad_copy = pltpu.make_async_copy(grad_hbm, grad, in_sem.at[2])
    own_shard.start()
    q_copy.start()
    grad_copy.start()

    def column(d):
        return xor(my_tile, d, tiles) * 2 + side

    barrier = pltpu.get_barrier_semaphore()
    pl.semaphore_signal(barrier, inc=1, device_id={"blk": neighbour}, device_id_type=MESH)
    for d in range(1, tiles):
        pl.semaphore_signal(barrier, inc=1, device_id={"blk": column(d)}, device_id_type=MESH)

    @pl.when(has_prev)
    def _():
        pl.semaphore_signal(barrier, inc=1, device_id={"grp": group - 1}, device_id_type=MESH)

    @pl.when(has_next)
    def _():
        pl.semaphore_signal(barrier, inc=1, device_id={"grp": group + 1}, device_id_type=MESH)

    own_shard.wait()
    if groups == 2:
        pl.semaphore_wait(barrier, tiles + 1)
    else:
        ends = jnp.minimum(group, 1) + jnp.minimum(groups - 1 - group, 1)
        pl.semaphore_wait(barrier, tiles + ends)

    def shard(j):
        return kv.at[pl.ds(block + j * rows, rows)]

    def spread(d, source, target):
        return pltpu.make_async_remote_copy(
            src_ref=shard(source),
            dst_ref=shard(source),
            send_sem=gat_send.at[d],
            recv_sem=gat_recv.at[source],
            device_id={"blk": target},
            device_id_type=MESH,
        )

    def hop(tile, j):
        return pltpu.make_async_remote_copy(
            src_ref=shard(j),
            dst_ref=shard(j),
            send_sem=hop_send.at[tile],
            recv_sem=gat_recv.at[j],
            device_id={"blk": neighbour},
            device_id_type=MESH,
        )

    def forward(j, to):
        return pltpu.make_async_remote_copy(
            src_ref=kv.at[pl.ds(block + j * rows, rows)],
            dst_ref=kv.at[pl.ds(j * rows, rows)],
            send_sem=fwd_send.at[j],
            recv_sem=fwd_recv.at[j],
            device_id={"grp": to},
            device_id_type=MESH,
        )

    def prev_terms(tile, to):
        return pltpu.make_async_remote_copy(
            src_ref=prev_part.at[pl.ds(tile * TILE, TILE)],
            dst_ref=next_part.at[pl.ds(tile * TILE, TILE)],
            send_sem=pp_send.at[tile],
            recv_sem=pp_recv.at[tile],
            device_id={"grp": to},
            device_id_type=MESH,
        )

    def pair(tile):
        return pltpu.make_async_remote_copy(
            src_ref=pair_part.at[tile],
            dst_ref=pair_in.at[tile],
            send_sem=pair_send.at[tile],
            recv_sem=pair_recv.at[tile],
            device_id={"blk": neighbour},
            device_id_type=MESH,
        )

    def reduce(source, target):
        return pltpu.make_async_remote_copy(
            src_ref=part.at[target],
            dst_ref=red.at[source],
            send_sem=red_send.at[target],
            recv_sem=red_recv.at[source],
            device_id={"blk": target * 2 + side},
            device_id_type=MESH,
        )

    hop(my_tile, me).start()
    for d in range(1, tiles):
        spread(d, me, column(d)).start()

    @pl.when(has_next)
    def _():
        forward(me, group + 1).start()

    q_copy.wait()
    grad_copy.wait()

    key_in_tile = lax.broadcasted_iota(jnp.int32, (TILE, block), 0)
    token = lax.broadcasted_iota(jnp.int32, (TILE, block), 1)

    def scores_of(start, visible, largest):
        at = pl.ds(pl.multiple_of(start, TILE), TILE)
        keys = kv[at, :]
        tile_s = jnp.where(visible, dot_nn(keys, q[...]) * score_scale, HIDDEN)
        dp[at, :] = dot_nt(keys[:, :rank], grad[...])
        top = jnp.max(tile_s, axis=0, keepdims=True)
        e = jnp.exp(tile_s - top)
        s[at, :] = e
        tops[start // TILE] = top
        sums[start // TILE] = jnp.sum(e, axis=0, keepdims=True)
        return jnp.maximum(largest, top)

    def relay(step):
        tile = xor(my_tile, step, tiles)
        j = tile * 2 + side
        spread(0, j, j).wait_recv()
        hop(tile, j).start()

        @pl.when(has_next)
        def _():
            forward(j, group + 1).start()

    def own_scores(step, largest):
        @pl.when(step == 0)
        def _():
            for later in range(1, tiles):
                relay(later)

        tile = xor(my_tile, step, tiles)
        j = tile * 2 + 1 - side
        hop(tile, j).wait_recv()

        @pl.when(has_next)
        def _():
            forward(j, group + 1).start()

        return scores_of(block + tile * TILE, tile * TILE + key_in_tile <= token, largest)

    def prev_scores(step, largest):
        tile = xor(my_tile, step, tiles)
        for j in (tile * 2, tile * 2 + 1):
            forward(j, group - 1).wait_recv()
        position = (group - 1) * block + tile * TILE + key_in_tile
        return scores_of(tile * TILE, position >= first_ref[...], largest)

    largest = jnp.full((1, block), HIDDEN, jnp.float32)
    largest = lax.fori_loop(0, tiles, own_scores, largest)
    largest = lax.fori_loop(0, prev_tiles, prev_scores, largest)

    def tile_rows(i):
        return pl.ds(pl.multiple_of(i * TILE, TILE), TILE)

    def rescale(i, total):
        factor = jnp.exp(tops[i] - largest)
        tops[i] = factor
        return total + factor * sums[i]

    zero = jnp.zeros((1, block), jnp.float32)
    first_tile = tiles - prev_tiles
    inverse = 1.0 / lax.fori_loop(first_tile, 2 * tiles, rescale, zero)

    def probs(i, delta):
        at = tile_rows(i)
        tile_p = (s[at, :] * (tops[i] * inverse)).astype(jnp.bfloat16)
        p[at, :] = tile_p
        return delta + jnp.sum(tile_p.astype(jnp.float32) * dp[at, :], axis=0, keepdims=True)

    delta = lax.fori_loop(first_tile, 2 * tiles, probs, zero)

    def score_grads(at):
        tile_d = p[at, :].astype(jnp.float32) * (dp[at, :] - delta) * score_scale
        ds[at, :] = tile_d.astype(jnp.bfloat16)

    def latent_terms(start):
        at = pl.ds(pl.multiple_of(start, TILE), TILE)
        score_grads(at)
        acc[...] = dot_nt(ds[at, :], q[...])
        acc[:, :rank] += dot_nn(p[at, :], grad[...])

    def prev_latents(step, carry):
        tile = xor(my_tile, tiles - 1 - step, tiles)
        latent_terms(tile * TILE)
        prev_part[pl.ds(pl.multiple_of(tile * TILE, TILE), TILE), :] = acc[...].astype(jnp.bfloat16)
        prev_terms(tile, group - 1).start()
        return carry

    lax.fori_loop(0, prev_tiles, prev_latents, 0)

    def query_grads():
        for start in range(0, block, 256):
            cut = slice(start, min(start + 256, block))

            @pl.when(has_prev)
            def _():
                dq[:, cut] = dot_tn(kv[...], ds[:, cut]).astype(jnp.bfloat16)

            @pl.when(group == 0)
            def _():
                dq[:, cut] = dot_tn(kv[block:, :], ds[block:, cut]).astype(jnp.bfloat16)

        pltpu.make_async_copy(dq, dq_hbm, out_sem).start()

    @pl.when(has_next)
    def _():
        for i in range(tiles, 2 * tiles):
            score_grads(pl.ds(i * TILE, TILE))
        query_grads()

    def pair_sum(step):
        tile = xor(my_tile, step, tiles)
        pair(tile).wait_recv()
        keep[tile] += pair_in[tile].astype(jnp.float32)

        @pl.when(tile != my_tile)
        def _():
            part[tile] = keep[tile].astype(jnp.bfloat16)
            reduce(my_tile, tile).start()

    def own_latents(i, carry):
        step = tiles - 1 - i
        tile = xor(my_tile, step, tiles)
        at = pl.ds(pl.multiple_of(tile * TILE, TILE), TILE)
        latent_terms(block + tile * TILE)

        @pl.when(has_next)
        def _():
            prev_terms(tile, group + 1).wait_recv()
            acc[...] += next_part[at, :].astype(jnp.float32)

        theirs = pl.ds(pl.multiple_of((1 - side) * rows, rows), rows)
        mine = pl.ds(pl.multiple_of(side * rows, rows), rows)
        pair_part[tile] = acc[theirs, :].astype(jnp.bfloat16)
        pair(tile).start()
        keep[tile] = acc[mine, :]

        @pl.when(i > 0)
        def _():
            pair_sum(step + 1)

        return carry

    lax.fori_loop(0, tiles, own_latents, 0)

    @pl.when(group == groups - 1)
    def _():
        query_grads()

    pair_sum(0)
    total = keep[my_tile]
    for d in range(1, tiles):
        source = xor(my_tile, d, tiles)
        reduce(source, my_tile).wait_recv()
        total = total + red[source].astype(jnp.float32)
    dl_ref[...] = total.astype(dl_ref.dtype)

    pltpu.make_async_copy(dq, dq_hbm, out_sem).wait()
    for tile in range(tiles):
        hop(tile, tile * 2 + side).wait_send()
        pair(tile).wait_send()
    for d in range(1, tiles):
        spread(d, me, column(d)).wait_send()
        reduce(my_tile, xor(my_tile, d, tiles)).wait_send()

    @pl.when(has_next)
    def _():
        for j in range(count):
            forward(j, group + 1).wait_send()

    @pl.when(has_prev)
    def _():
        for tile in range(tiles):
            prev_terms(tile, group - 1).wait_send()


def fits(count, block, head_local):
    rows = block // count
    tiles = block // TILE
    powers = count & (count - 1) == 0 and tiles & (tiles - 1) == 0
    return head_local == 1 and rows % 16 == 0 and TILE == 2 * rows and block % TILE == 0 and powers


def shards(queries, latents, out_grad, first_key):
    block, head_local, width = queries.shape
    rank = out_grad.shape[2]
    count, groups = lax.axis_size("blk"), lax.axis_size("grp")
    if not fits(count, block, head_local):
        return shards_by_collectives(queries, latents, out_grad, first_key)
    rows, tiles = block // count, block // TILE
    bf16, f32 = jnp.bfloat16, jnp.float32
    dma = pltpu.SemaphoreType.DMA
    anywhere = pl.BlockSpec(memory_space=pltpu.HBM)
    vmem = pl.BlockSpec(memory_space=pltpu.VMEM)
    query_grad, latent_grad = pl.pallas_call(
        functools.partial(kernel, groups, count),
        out_shape=(
            jax.ShapeDtypeStruct((width, block), bf16),
            jax.ShapeDtypeStruct((rows, width), bf16),
        ),
        in_specs=[anywhere, anywhere, anywhere, vmem],
        out_specs=(anywhere, vmem),
        scratch_shapes=[
            pltpu.VMEM((width, block), bf16),
            pltpu.VMEM((block, rank), bf16),
            pltpu.VMEM((2 * block, width), bf16),
            pltpu.VMEM((2 * block, block), f32),
            pltpu.VMEM((2 * block, block), f32),
            pltpu.VMEM((2 * block, block), bf16),
            pltpu.VMEM((2 * block, block), bf16),
            pltpu.VMEM((width, block), bf16),
            pltpu.VMEM((2 * tiles, 1, block), f32),
            pltpu.VMEM((2 * tiles, 1, block), f32),
            pltpu.VMEM((TILE, width), f32),
            pltpu.VMEM((tiles, rows, width), f32),
            pltpu.VMEM((tiles, rows, width), bf16),
            pltpu.VMEM((tiles, rows, width), bf16),
            pltpu.VMEM((tiles, rows, width), bf16),
            pltpu.VMEM((tiles, rows, width), bf16),
            pltpu.VMEM((block, width), bf16),
            pltpu.VMEM((block, width), bf16),
            dma((3,)),
            dma((tiles,)),
            dma((tiles,)),
            dma((count,)),
            dma((count,)),
            dma((count,)),
            dma((tiles,)),
            dma((tiles,)),
            dma((tiles,)),
            dma((tiles,)),
            dma((tiles,)),
            dma((tiles,)),
            dma,
        ],
        compiler_params=pltpu.CompilerParams(
            collective_id=0, has_side_effects=True, vmem_limit_bytes=40 * 1024 * 1024
        ),
    )(
        pltpu.with_memory_space_constraint(queries.reshape(block, width).T, pltpu.HBM),
        latents,
        pltpu.with_memory_space_constraint(out_grad.reshape(block, rank), pltpu.HBM),
        first_key.reshape(1, block),
    )
    return (query_grad.T.reshape(block, 1, width), latent_grad)


def solution(mesh):
    placed = (
        P(("rep", "grp"), "blk", None),
        P(("rep", "grp", "blk"), None),
        P(("rep", "grp"), "blk", None),
        P(("rep", "grp")),
    )
    return jax.shard_map(
        shards,
        mesh=mesh,
        in_specs=placed,
        out_specs=(P(("rep", "grp"), "blk", None), P(("rep", "grp", "blk"), None)),
        check_vma=False,
    )
```

```python
import functools

import jax
import jax.numpy as jnp
from jax import lax
from jax.experimental import pallas as pl
from jax.experimental.pallas import tpu as pltpu
from jax.sharding import PartitionSpec as P

score_scale = 192.0 ** (-0.5)


def shifted(shard, axis, by):
    count = lax.axis_size(axis)
    pairs = [(i, i + by) for i in range(count) if 0 <= i + by < count]
    return lax.ppermute(shard, axis, pairs)


def attend_grads(query_blk, grad_blk, key_rows, visible):
    count, head_count, width = query_blk.shape
    query_rows = query_blk.reshape(count * head_count, width)
    grad_rows = grad_blk.reshape(count * head_count, -1)
    rank_width = grad_rows.shape[1]
    value_rows = key_rows[:, :rank_width]
    scores = jnp.dot(query_rows, key_rows.T, preferred_element_type=jnp.float32) * score_scale
    scores = scores.reshape(count, head_count, -1)
    mask_three = visible[:, None, :]
    row_max = jnp.max(jnp.where(mask_three, scores, -jnp.inf), axis=-1, keepdims=True)
    total = jnp.sum(jnp.where(mask_three, jnp.exp(scores - row_max), 0.0), axis=-1, keepdims=True)
    log_norm = row_max + jnp.log(total)
    attn_probs = jnp.where(mask_three, jnp.exp(scores - log_norm), 0.0).astype(jnp.bfloat16)
    attn_probs = attn_probs.reshape(count * head_count, -1)
    outputs = jnp.dot(attn_probs, value_rows, preferred_element_type=jnp.float32)
    row_delta = jnp.sum(grad_rows.astype(jnp.float32) * outputs, axis=-1, keepdims=True)
    prob_grad = jnp.dot(grad_rows, value_rows.T, preferred_element_type=jnp.float32)
    score_grad = (attn_probs.astype(jnp.float32) * (prob_grad - row_delta) * score_scale).astype(
        jnp.bfloat16
    )
    query_grad = jnp.dot(score_grad, key_rows, preferred_element_type=jnp.float32).astype(
        jnp.bfloat16
    )
    latent_part = jnp.dot(score_grad.T, query_rows, preferred_element_type=jnp.float32)
    value_part = jnp.dot(attn_probs.T, grad_rows, preferred_element_type=jnp.float32)
    latent_part = jnp.concatenate(
        [latent_part[:, :rank_width] + value_part, latent_part[:, rank_width:]], axis=1
    )
    return (query_grad.reshape(count, head_count, width), latent_part)


def shards_by_collectives(queries, latents, out_grad, first_key):
    block_len = queries.shape[0]
    head_local = queries.shape[1]
    width = queries.shape[2]
    rank_width = out_grad.shape[2]
    group_index = lax.axis_index("grp")
    own_block = lax.all_gather(latents, "blk", axis=0, tiled=True)
    prev_block = shifted(own_block, "grp", 1)
    key_rows = jnp.concatenate([prev_block, own_block], axis=0)
    key_iota = jnp.arange(2 * block_len, dtype=jnp.int32)
    key_pos = key_iota + (group_index - 1) * block_len
    in_prev = key_iota < block_len
    piece = min(512, block_len)
    pieces = block_len // piece
    query_steps = queries.reshape(pieces, piece, head_local, width)
    grad_steps = out_grad.reshape(pieces, piece, head_local, rank_width)
    first_steps = first_key.reshape(pieces, piece)
    pos_steps = (jnp.arange(block_len, dtype=jnp.int32) + group_index * block_len).reshape(
        pieces, piece
    )

    def scan_step(carry, items):
        query_blk, grad_blk, first_blk, pos_blk = items
        prev_ok = (key_pos[None, :] >= first_blk[:, None]) & (group_index > 0)
        own_ok = key_pos[None, :] <= pos_blk[:, None]
        visible = jnp.where(in_prev[None, :], prev_ok, own_ok)
        query_part, latent_part = attend_grads(query_blk, grad_blk, key_rows, visible)
        return (carry + latent_part, query_part)

    carry_init = jnp.zeros((2 * block_len, width), jnp.float32)
    latent_part, query_blocks = lax.scan(
        scan_step, carry_init, (query_steps, grad_steps, first_steps, pos_steps)
    )
    query_grad = query_blocks.reshape(block_len, head_local, width)
    prev_part = latent_part[:block_len]
    own_part = latent_part[block_len:]
    from_later = shifted(prev_part.astype(jnp.bfloat16), "grp", -1).astype(prev_part.dtype)
    latent_total = lax.psum_scatter(own_part + from_later, "blk", scatter_dimension=0, tiled=True)
    return (query_grad, latent_total.astype(jnp.bfloat16))


MESH = pl.DeviceIdType.MESH
TILE = 128
HIDDEN = -1e30


def xor(a, b, count):
    out, bit = 0, 1
    while bit < count:
        out = out + bit * ((a // bit + b // bit) % 2)
        bit *= 2
    return out


def dot_nt(a, b):
    return lax.dot_general(a, b, (((1,), (1,)), ((), ())), preferred_element_type=jnp.float32)


def dot_tn(a, b):
    return lax.dot_general(a, b, (((0,), (0,)), ((), ())), preferred_element_type=jnp.float32)


def dot_nn(a, b):
    return jnp.dot(a, b, preferred_element_type=jnp.float32)


def kernel(
    groups, count, q_hbm, lat_hbm, grad_hbm, first_ref, dq_hbm, dl_ref,
    q, grad, kv, s, dp, p, ds, dq, tops, sums, acc, keep, pair_part, pair_in, part, red, prev_part, next_part,
    in_sem, gat_send, hop_send, gat_recv, fwd_send, fwd_recv, pp_send, pp_recv,
    pair_send, pair_recv, red_send, red_recv, out_sem,
):
    width, block = q.shape
    rank = grad.shape[1]
    rows = block // count
    tiles = block // TILE
    me = lax.axis_index("blk")
    group = lax.axis_index("grp")
    has_prev = group > 0
    has_next = group < groups - 1
    my_tile, side = me // 2, me % 2
    neighbour = my_tile * 2 + 1 - side
    prev_tiles = tiles * jnp.minimum(group, 1)

    own_shard = pltpu.make_async_copy(lat_hbm, kv.at[pl.ds(block + me * rows, rows)], in_sem.at[0])
    q_copy = pltpu.make_async_copy(q_hbm, q, in_sem.at[1])
    grad_copy = pltpu.make_async_copy(grad_hbm, grad, in_sem.at[2])
    own_shard.start()
    q_copy.start()
    grad_copy.start()

    def column(d):
        return xor(my_tile, d, tiles) * 2 + side

    barrier = pltpu.get_barrier_semaphore()
    pl.semaphore_signal(barrier, inc=1, device_id={"blk": neighbour}, device_id_type=MESH)
    for d in range(1, tiles):
        pl.semaphore_signal(barrier, inc=1, device_id={"blk": column(d)}, device_id_type=MESH)

    @pl.when(has_prev)
    def _():
        pl.semaphore_signal(barrier, inc=1, device_id={"grp": group - 1}, device_id_type=MESH)

    @pl.when(has_next)
    def _():
        pl.semaphore_signal(barrier, inc=1, device_id={"grp": group + 1}, device_id_type=MESH)

    own_shard.wait()
    if groups == 2:
        pl.semaphore_wait(barrier, tiles + 1)
    else:
        ends = jnp.minimum(group, 1) + jnp.minimum(groups - 1 - group, 1)
        pl.semaphore_wait(barrier, tiles + ends)

    def shard(j):
        return kv.at[pl.ds(block + j * rows, rows)]

    def spread(d, source, target):
        return pltpu.make_async_remote_copy(
            src_ref=shard(source),
            dst_ref=shard(source),
            send_sem=gat_send.at[d],
            recv_sem=gat_recv.at[source],
            device_id={"blk": target},
            device_id_type=MESH,
        )

    def hop(tile, j):
        return pltpu.make_async_remote_copy(
            src_ref=shard(j),
            dst_ref=shard(j),
            send_sem=hop_send.at[tile],
            recv_sem=gat_recv.at[j],
            device_id={"blk": neighbour},
            device_id_type=MESH,
        )

    def forward(j, to):
        return pltpu.make_async_remote_copy(
            src_ref=kv.at[pl.ds(block + j * rows, rows)],
            dst_ref=kv.at[pl.ds(j * rows, rows)],
            send_sem=fwd_send.at[j],
            recv_sem=fwd_recv.at[j],
            device_id={"grp": to},
            device_id_type=MESH,
        )

    def prev_terms(tile, to):
        return pltpu.make_async_remote_copy(
            src_ref=prev_part.at[pl.ds(tile * TILE, TILE)],
            dst_ref=next_part.at[pl.ds(tile * TILE, TILE)],
            send_sem=pp_send.at[tile],
            recv_sem=pp_recv.at[tile],
            device_id={"grp": to},
            device_id_type=MESH,
        )

    def pair(tile):
        return pltpu.make_async_remote_copy(
            src_ref=pair_part.at[tile],
            dst_ref=pair_in.at[tile],
            send_sem=pair_send.at[tile],
            recv_sem=pair_recv.at[tile],
            device_id={"blk": neighbour},
            device_id_type=MESH,
        )

    def reduce(source, target):
        return pltpu.make_async_remote_copy(
            src_ref=part.at[target],
            dst_ref=red.at[source],
            send_sem=red_send.at[target],
            recv_sem=red_recv.at[source],
            device_id={"blk": target * 2 + side},
            device_id_type=MESH,
        )

    hop(my_tile, me).start()
    for d in range(1, tiles):
        spread(d, me, column(d)).start()

    @pl.when(has_next)
    def _():
        forward(me, group + 1).start()

    q_copy.wait()
    grad_copy.wait()

    key_in_tile = lax.broadcasted_iota(jnp.int32, (TILE, block), 0)
    token = lax.broadcasted_iota(jnp.int32, (TILE, block), 1)

    def scores_of(start, visible, largest):
        at = pl.ds(pl.multiple_of(start, TILE), TILE)
        keys = kv[at, :]
        tile_s = jnp.where(visible, dot_nn(keys, q[...]) * score_scale, HIDDEN)
        dp[at, :] = dot_nt(keys[:, :rank], grad[...])
        top = jnp.max(tile_s, axis=0, keepdims=True)
        e = jnp.exp(tile_s - top)
        s[at, :] = e
        tops[start // TILE] = top
        sums[start // TILE] = jnp.sum(e, axis=0, keepdims=True)
        return jnp.maximum(largest, top)

    def relay(step):
        tile = xor(my_tile, step, tiles)
        j = tile * 2 + side
        spread(0, j, j).wait_recv()
        hop(tile, j).start()

        @pl.when(has_next)
        def _():
            forward(j, group + 1).start()

    def own_scores(step, largest):
        @pl.when(step == 0)
        def _():
            for later in range(1, tiles):
                relay(later)

        tile = xor(my_tile, step, tiles)
        j = tile * 2 + 1 - side
        hop(tile, j).wait_recv()

        @pl.when(has_next)
        def _():
            forward(j, group + 1).start()

        return scores_of(block + tile * TILE, tile * TILE + key_in_tile <= token, largest)

    def prev_scores(step, largest):
        tile = xor(my_tile, step, tiles)
        for j in (tile * 2, tile * 2 + 1):
            forward(j, group - 1).wait_recv()
        position = (group - 1) * block + tile * TILE + key_in_tile
        return scores_of(tile * TILE, position >= first_ref[...], largest)

    largest = jnp.full((1, block), HIDDEN, jnp.float32)
    largest = lax.fori_loop(0, tiles, own_scores, largest)
    largest = lax.fori_loop(0, prev_tiles, prev_scores, largest)

    def tile_rows(i):
        return pl.ds(pl.multiple_of(i * TILE, TILE), TILE)

    def rescale(i, total):
        factor = jnp.exp(tops[i] - largest)
        tops[i] = factor
        return total + factor * sums[i]

    zero = jnp.zeros((1, block), jnp.float32)
    first_tile = tiles - prev_tiles
    inverse = 1.0 / lax.fori_loop(first_tile, 2 * tiles, rescale, zero)

    def probs(i, delta):
        at = tile_rows(i)
        tile_p = (s[at, :] * (tops[i] * inverse)).astype(jnp.bfloat16)
        p[at, :] = tile_p
        return delta + jnp.sum(tile_p.astype(jnp.float32) * dp[at, :], axis=0, keepdims=True)

    delta = lax.fori_loop(first_tile, 2 * tiles, probs, zero)

    def score_grads(at):
        tile_d = p[at, :].astype(jnp.float32) * (dp[at, :] - delta) * score_scale
        ds[at, :] = tile_d.astype(jnp.bfloat16)

    def latent_terms(start):
        at = pl.ds(pl.multiple_of(start, TILE), TILE)
        score_grads(at)
        acc[...] = dot_nt(ds[at, :], q[...])
        acc[:, :rank] += dot_nn(p[at, :], grad[...])

    def prev_latents(step, carry):
        tile = xor(my_tile, tiles - 1 - step, tiles)
        latent_terms(tile * TILE)
        prev_part[pl.ds(pl.multiple_of(tile * TILE, TILE), TILE), :] = acc[...].astype(jnp.bfloat16)
        prev_terms(tile, group - 1).start()
        return carry

    lax.fori_loop(0, prev_tiles, prev_latents, 0)

    def query_grads():
        for start in range(0, block, 256):
            cut = slice(start, min(start + 256, block))

            @pl.when(has_prev)
            def _():
                dq[:, cut] = dot_tn(kv[...], ds[:, cut]).astype(jnp.bfloat16)

            @pl.when(group == 0)
            def _():
                dq[:, cut] = dot_tn(kv[block:, :], ds[block:, cut]).astype(jnp.bfloat16)

        pltpu.make_async_copy(dq, dq_hbm, out_sem).start()

    @pl.when(has_next)
    def _():
        for i in range(tiles, 2 * tiles):
            score_grads(pl.ds(i * TILE, TILE))
        query_grads()

    def pair_sum(step):
        tile = xor(my_tile, step, tiles)
        pair(tile).wait_recv()
        keep[tile] += pair_in[tile].astype(jnp.float32)

        @pl.when(tile != my_tile)
        def _():
            part[tile] = keep[tile].astype(jnp.bfloat16)
            reduce(my_tile, tile).start()

    def own_latents(i, carry):
        step = tiles - 1 - i
        tile = xor(my_tile, step, tiles)
        at = pl.ds(pl.multiple_of(tile * TILE, TILE), TILE)
        latent_terms(block + tile * TILE)

        @pl.when(has_next)
        def _():
            prev_terms(tile, group + 1).wait_recv()
            acc[...] += next_part[at, :].astype(jnp.float32)

        theirs = pl.ds(pl.multiple_of((1 - side) * rows, rows), rows)
        mine = pl.ds(pl.multiple_of(side * rows, rows), rows)
        pair_part[tile] = acc[theirs, :].astype(jnp.bfloat16)
        pair(tile).start()
        keep[tile] = acc[mine, :]

        @pl.when(i > 0)
        def _():
            pair_sum(step + 1)

        return carry

    lax.fori_loop(0, tiles, own_latents, 0)

    @pl.when(group == groups - 1)
    def _():
        query_grads()

    pair_sum(0)
    total = keep[my_tile]
    for d in range(1, tiles):
        source = xor(my_tile, d, tiles)
        reduce(source, my_tile).wait_recv()
        total = total + red[source].astype(jnp.float32)
    dl_ref[...] = total.astype(dl_ref.dtype)

    pltpu.make_async_copy(dq, dq_hbm, out_sem).wait()
    for tile in range(tiles):
        hop(tile, tile * 2 + side).wait_send()
        pair(tile).wait_send()
    for d in range(1, tiles):
        spread(d, me, column(d)).wait_send()
        reduce(my_tile, xor(my_tile, d, tiles)).wait_send()

    @pl.when(has_next)
    def _():
        for j in range(count):
            forward(j, group + 1).wait_send()

    @pl.when(has_prev)
    def _():
        for tile in range(tiles):
            prev_terms(tile, group - 1).wait_send()


def fits(count, block, head_local):
    rows = block // count
    tiles = block // TILE
    powers = count & (count - 1) == 0 and tiles & (tiles - 1) == 0
    return head_local == 1 and rows % 16 == 0 and TILE == 2 * rows and block % TILE == 0 and powers


def shards(queries, latents, out_grad, first_key):
    block, head_local, width = queries.shape
    rank = out_grad.shape[2]
    count, groups = lax.axis_size("blk"), lax.axis_size("grp")
    if not fits(count, block, head_local):
        return shards_by_collectives(queries, latents, out_grad, first_key)
    rows, tiles = block // count, block // TILE
    bf16, f32 = jnp.bfloat16, jnp.float32
    dma = pltpu.SemaphoreType.DMA
    anywhere = pl.BlockSpec(memory_space=pltpu.HBM)
    vmem = pl.BlockSpec(memory_space=pltpu.VMEM)
    query_grad, latent_grad = pl.pallas_call(
        functools.partial(kernel, groups, count),
        out_shape=(
            jax.ShapeDtypeStruct((width, block), bf16),
            jax.ShapeDtypeStruct((rows, width), bf16),
        ),
        in_specs=[anywhere, anywhere, anywhere, vmem],
        out_specs=(anywhere, vmem),
        scratch_shapes=[
            pltpu.VMEM((width, block), bf16),
            pltpu.VMEM((block, rank), bf16),
            pltpu.VMEM((2 * block, width), bf16),
            pltpu.VMEM((2 * block, block), f32),
            pltpu.VMEM((2 * block, block), f32),
            pltpu.VMEM((2 * block, block), bf16),
            pltpu.VMEM((2 * block, block), bf16),
            pltpu.VMEM((width, block), bf16),
            pltpu.VMEM((2 * tiles, 1, block), f32),
            pltpu.VMEM((2 * tiles, 1, block), f32),
            pltpu.VMEM((TILE, width), f32),
            pltpu.VMEM((tiles, rows, width), f32),
            pltpu.VMEM((tiles, rows, width), bf16),
            pltpu.VMEM((tiles, rows, width), bf16),
            pltpu.VMEM((tiles, rows, width), bf16),
            pltpu.VMEM((tiles, rows, width), bf16),
            pltpu.VMEM((block, width), bf16),
            pltpu.VMEM((block, width), bf16),
            dma((3,)),
            dma((tiles,)),
            dma((tiles,)),
            dma((count,)),
            dma((count,)),
            dma((count,)),
            dma((tiles,)),
            dma((tiles,)),
            dma((tiles,)),
            dma((tiles,)),
            dma((tiles,)),
            dma((tiles,)),
            dma,
        ],
        compiler_params=pltpu.CompilerParams(
            collective_id=0, has_side_effects=True, vmem_limit_bytes=40 * 1024 * 1024
        ),
    )(
        pltpu.with_memory_space_constraint(queries.reshape(block, width).T, pltpu.HBM),
        pltpu.with_memory_space_constraint(latents, pltpu.HBM),
        pltpu.with_memory_space_constraint(out_grad.reshape(block, rank), pltpu.HBM),
        first_key.reshape(1, block),
    )
    return (query_grad.T.reshape(block, 1, width), latent_grad)


def solution(mesh):
    placed = (
        P(("rep", "grp"), "blk", None),
        P(("rep", "grp", "blk"), None),
        P(("rep", "grp"), "blk", None),
        P(("rep", "grp")),
    )
    return jax.shard_map(
        shards,
        mesh=mesh,
        in_specs=placed,
        out_specs=(P(("rep", "grp"), "blk", None), P(("rep", "grp", "blk"), None)),
        check_vma=False,
    )
```
